512 devices in a mesh: energy: 8 (over y_lo, x), contour: 64 (over z, y_hi, core).
Axes of the slice: x: 4, y: 4 (y_hi: 2, y_lo: 2; y = y_hi * 2 + y_lo), z: 16, core: 2. Of those that a mesh axis runs over, the one named last changes fastest.
Arguments:
- energies: float32 [16], P('energy'), may hold values from -0.05 to 0.05
- onsite: float32 [4096], replicated, may hold values from -1.6 to 1.6, as said below
- blocks: bfloat16 [32, 3, 128, 128], replicated, may hold values from -0.09375 to 0.09375
- pattern: int32 [32, 3], replicated, may hold values from 0 to 31, all different within a row
- probes: bfloat16 [64, 4096], replicated, may hold values from -6 to 6
- ranks: int32 [16], P('energy'), may hold values from 16 to 64
- owner_map: int32 [16, 1], replicated, may hold values from 0 to 7, as said below
Outputs:
- sigma_owned: bfloat16 [8, 3, 2, 512, 512], P('energy', None, None, 'contour')
The draws below stay inside these ranges and needn't reach their ends.
Inputs may be any that keep to these rules, and one draw needn't show every extreme that they name: `onsite`: every value lies within 0.5 of zero or between 1.12 and 1.6 in magnitude. `pattern`: each row lists 3 different block columns. `owner_map`: every owner group receives at least one energy and at most 3, and some owner receives exactly 3; some energy group (aligned blocks of 2 rows) sends both its energies to one owner.
All inputs are finite; a program needn't handle non-finite values.
Results may differ from the reference program's by a relative error of at most 0.0022.
Values may be sent and summed in bfloat16 or wider, within the bound.
No kernel may reach another device: no remote copies, remote signals or barrier semaphores. Data moves between devices by JAX's collectives and lax.ppermute only.
A program may use at most 64 MiB of HBM per device.

```python
import math
import jax
import jax.numpy as jnp
from jax import lax

NB = 4096
BS = 128
NBR = 32
KB = 3
L = 64
NC = 512
SWEEPS = 2
E_DEV = 2
ENERGIES = 16
OWNERS = 8
CAPE = 3
N_CONTOUR = 64


def draw_onsite(key, part):
    key = jax.random.fold_in(key, 11)
    pick_key, inner_key, outer_key, sign_key = jax.random.split(key, 4)
    inner_share = 0.5
    picked = jax.random.uniform(pick_key, (NB,), jnp.float32)
    inner_values = jax.random.uniform(inner_key, (NB,), jnp.float32, -0.5, 0.5)
    outer_values = jax.random.uniform(outer_key, (NB,), jnp.float32, 1.12, 1.6)
    signs = jnp.where(jax.random.uniform(sign_key, (NB,), jnp.float32) < 0.5, -1.0, 1.0)
    return jnp.where(picked < inner_share, inner_values, signs * outer_values).astype(jnp.float32)


def draw_owner_map(key, part):
    key = jax.random.fold_in(key, 23)
    group_key, owner_key, move_key = jax.random.split(key, 3)
    group_order = jax.random.permutation(group_key, OWNERS)
    owner_order = jax.random.permutation(owner_key, OWNERS)
    labels = jnp.arange(OWNERS)
    coins = jax.random.randint(move_key, (OWNERS,), 0, 2)
    moved_slot = jnp.where(labels == 0, 1, jnp.where(labels == OWNERS - 1, 0, coins))
    energy_index = jnp.arange(ENERGIES)
    group = energy_index // E_DEV
    within = energy_index % E_DEV
    start_slot = group_order[group]
    within = jnp.where((moved_slot[start_slot] == 1) & (within == 1), 0, within)
    base = (start_slot + within) % OWNERS
    return owner_order[base].reshape(ENERGIES, 1).astype(jnp.int32)


def plant(values, key, smallest, largest):
    longest = values.shape.index(max(values.shape))
    spots = []
    for shift in (0, 1):
        where = [jax.random.randint(jax.random.fold_in(key, axis), (), 0, length) for axis, length in enumerate(values.shape)]
        where[longest] = (where[longest] + shift) % values.shape[longest]
        spots.append(tuple(where))
    return values.at[spots[0]].set(smallest).at[spots[1]].set(largest)


def shard_levels(key, dims, cuts, least, largest):
    def one(dim, blocks):
        draws = jax.random.uniform(jax.random.fold_in(jax.random.fold_in(key, 6), dim), (blocks,), jnp.float32, least / len(cuts), largest / len(cuts))
        return jnp.repeat(jnp.exp(draws), dims[dim] // blocks).reshape((-1,) + (1,) * (len(dims) - dim - 1))

    gain = one(*cuts[0])
    for cut in cuts[1:]:
        gain = gain * one(*cut)
    return gain


def picks_of(rng, rows, amount, top, lift):
    sequence = jax.random.permutation(jax.random.fold_in(rng, 1), amount)
    pull = sequence
    for power in range(3):
        pull = pull * pull // amount
    pull = pull * lift // amount
    chance = jax.random.randint(jax.random.fold_in(rng, 2), (rows, amount), 0, 4096) + pull
    holders = jax.random.permutation(jax.random.fold_in(rng, 3), rows)[jnp.arange(amount) % rows]
    chance = jnp.where(jnp.arange(rows)[:, None] == holders[None, :], 1 << 14, chance)
    score = chance * amount + jnp.arange(amount)
    return lax.top_k(score.astype(jnp.int32), top)[1].astype(jnp.int32)


def noise(rng, shape, deviation, most, kind=jnp.bfloat16):
    return jnp.clip(deviation * jax.random.normal(rng, shape, jnp.float32), -most, most).astype(kind)


def setup_inputs(seed: int = 0) -> dict:
    key_of = jax.random.split(jax.random.key(seed), 8)
    energies = jnp.clip(jax.random.uniform(key_of[0], (ENERGIES,), jnp.float32, -0.05, 0.05) * shard_levels(key_of[0], (ENERGIES,), ((0, 8),), -0.4, 0.0), -0.05, 0.05)
    onsite = draw_onsite(jax.random.fold_in(key_of[7], 71), 0)
    blocks = noise(key_of[2], (NBR, KB, BS, BS), (0.12 / (KB * BS) ** 0.5), 0.09375)
    pattern = picks_of(key_of[3], NBR, NBR, KB, 0)
    probes = noise(key_of[4], (L, NB), 1.0, 6.0)
    ranks = plant(jax.random.randint(key_of[5], (ENERGIES,), L // 4, L + 1), jax.random.fold_in(key_of[5], 1), L // 4, L).astype(jnp.int32)
    owner_map = draw_owner_map(jax.random.fold_in(key_of[7], 71), 0)
    return dict(energies=energies, onsite=onsite, blocks=blocks, pattern=pattern, probes=probes, ranks=ranks, owner_map=owner_map)


highest = lax.Precision.HIGHEST

def inner(left, right):
    return lax.dot_general(left.astype(jnp.float32), right.astype(jnp.float32), (((1,), (1,)), ((), ())), precision=highest, preferred_element_type=jnp.float32)

def outer_first(left, right):
    return lax.dot_general(left.astype(jnp.float32), right.astype(jnp.float32), (((0,), (0,)), ((), ())), precision=highest, preferred_element_type=jnp.float32)

def gram_parts(first, second):
    gram_real = inner(first[0], first[0]) + inner(first[1], first[1])
    gram_imag = inner(first[0], first[1]) - inner(first[1], first[0])
    cross_real = inner(first[0], second[0]) + inner(first[1], second[1])
    cross_imag = inner(first[0], second[1]) - inner(first[1], second[0])
    return (jnp.stack([gram_real, gram_imag]), jnp.stack([cross_real, cross_imag]))

def solve_reduced(gram, cross, rows):
    size = gram.shape[1]
    identity_matrix = jnp.eye(size, dtype=jnp.float32)
    gram_real = gram[0] / rows + identity_matrix
    gram_imag = gram[1] / rows
    system = jnp.concatenate([jnp.concatenate([gram_real, -gram_imag], 1), jnp.concatenate([gram_imag, gram_real], 1)], 0)
    right_side = jnp.concatenate([cross[0], cross[1]], 0) / rows
    factor = jnp.linalg.cholesky(system)
    solved = jax.scipy.linalg.cho_solve((factor, True), right_side)
    return (solved[:size], solved[size:])

def sigma_rows(kernel_real, kernel_imag, second_rows, first_full, count):
    trans_real = outer_first(kernel_real, second_rows[0]) - outer_first(kernel_imag, second_rows[1])
    trans_imag = outer_first(kernel_real, second_rows[1]) + outer_first(kernel_imag, second_rows[0])
    sigma_real = outer_first(trans_real, first_full[0]) + outer_first(trans_imag, first_full[1])
    sigma_imag = outer_first(trans_imag, first_full[0]) - outer_first(trans_real, first_full[1])
    return (jnp.stack([sigma_real, sigma_imag]) / count).astype(jnp.bfloat16)

def reference(energies, onsite, blocks, pattern, probes, ranks, owner_map):
    points = N_CONTOUR
    theta = 2.0 * math.pi * (jnp.arange(points).astype(jnp.float32) + 0.5) / points
    source = probes.astype(jnp.float32)[None]
    blocks_wide = blocks.astype(jnp.float32)
    sigmas = []
    for energy_index in range(ENERGIES):
        real_shift = energies[energy_index] + jnp.cos(theta)[:, None] - onsite[None, :]
        imag_shift = jnp.sin(theta)[:, None] + jnp.zeros_like(onsite)[None, :]
        modulus = real_shift * real_shift + imag_shift * imag_shift
        inv_real = (real_shift / modulus)[:, None, :]
        inv_imag = (imag_shift / modulus)[:, None, :]
        real_part = source * inv_real
        imag_part = -source * inv_imag
        for repeat in range(SWEEPS - 1):
            stacked = jnp.stack([real_part, imag_part], 1).astype(jnp.bfloat16).astype(jnp.float32)
            stacked = stacked.reshape(points, 2, L, NBR, BS)
            picked = stacked[:, :, :, pattern, :]
            coupled = jnp.einsum('prlikb,ikab->prlia', picked, blocks_wide, precision=highest).reshape(points, 2, L, NB)
            sum_real = source + coupled[:, 0]
            sum_imag = coupled[:, 1]
            real_part = sum_real * inv_real + sum_imag * inv_imag
            imag_part = sum_imag * inv_real - sum_real * inv_imag
        real_near = real_part[:, :, :NC]
        imag_near = imag_part[:, :, :NC]
        moments = []
        for power in (1, 2):
            cosine = (jnp.cos(power * theta) / points)[:, None, None]
            sine = (jnp.sin(power * theta) / points)[:, None, None]
            moment_real = jnp.sum(cosine * real_near - sine * imag_near, 0)
            moment_imag = jnp.sum(cosine * imag_near + sine * real_near, 0)
            moments.append(jnp.stack([moment_real, moment_imag]))
        keep = (jnp.arange(L) < ranks[energy_index]).astype(jnp.float32)[None, :, None]
        first = moments[0] * keep
        second = moments[1] * keep
        gram, cross = gram_parts(first, second)
        kernel_real, kernel_imag = solve_reduced(gram, cross, NC)
        sigmas.append(sigma_rows(kernel_real, kernel_imag, second, first, L))
    sigma = jnp.stack(sigmas).reshape(ENERGIES, 2 * NC * NC).astype(jnp.float32)
    owners = owner_map[:, 0]
    placed = []
    for owner_index in range(OWNERS):
        mine = (owners == owner_index).astype(jnp.int32)
        slot_index = jnp.cumsum(mine) - mine
        selector = ((jnp.arange(CAPE)[:, None] == slot_index[None, :]) & (mine[None, :] == 1)).astype(jnp.float32)
        placed.append(jnp.dot(selector, sigma, precision=highest))
    return jnp.stack(placed).reshape(OWNERS, CAPE, 2, NC, NC).astype(jnp.bfloat16)
```

```python
import jax
import jax.numpy as jnp
from jax import lax
from jax.experimental import pallas as pl
from jax.experimental.pallas import tpu as pltpu
from jax.sharding import PartitionSpec as P


L = 64
NC = 512
BS = 128
KB = 3
NEAR = NC // BS

f32 = jnp.float32
bf16 = jnp.bfloat16


def dot_nt(left, right):
    return lax.dot_general(left, right, (((1,), (1,)), ((), ())), preferred_element_type=f32)


def dot_nn(left, right):
    return lax.dot_general(left, right, (((1,), (0,)), ((), ())), preferred_element_type=f32)


def split(x):
    high = x.astype(bf16)
    return high, (x - high.astype(f32)).astype(bf16)


def powers(base):
    out = [base]
    for _ in range(6):
        out.append(out[-1] * out[-1])
    return out


def sigma_kernel(
    energies_in, ranks_in, onsite_in, pattern_in, probes, blocks, out,
    energies, ranks, onsite, pattern, pr, bl, mix, terms, big, wide, sems,
):
    local = big.shape[0]
    small_copies = [
        pltpu.make_async_copy(source, target, sems.at[n])
        for n, (source, target) in enumerate(
            ((onsite_in, onsite), (pattern_in, pattern), (energies_in, energies), (ranks_in, ranks))
        )
    ]
    large_copies = [pltpu.make_async_copy(probes, pr, sems.at[4])]
    for k in range(KB):
        large_copies.append(
            pltpu.make_async_copy(
                blocks.at[pl.ds(0, NEAR), k], bl.at[:, :, pl.ds(k * BS, BS)], sems.at[5 + k]
            )
        )
    for copy in small_copies + large_copies:
        copy.start()
    position = lax.axis_index("contour")
    sub_index = lax.broadcasted_iota(jnp.int32, (8, BS), 0)
    lane_index = lax.broadcasted_iota(jnp.int32, (8, BS), 1)

    for copy in small_copies:
        copy.wait()
    columns = []
    for i in range(NEAR):
        columns.append(jnp.broadcast_to(onsite[pl.ds(i, 1), :], (BS, BS)).T)
    for copy in large_copies:
        copy.wait()

    for i in range(NEAR):
        for e in range(local):
            rows = []
            for k in range(KB):
                at = pattern[k, i]
                row = jnp.broadcast_to(onsite[pl.ds(at, 1), :], (8, BS)) - energies[e]
                raised = powers(row)
                rows.append(raised)
                weight = 1.0 / (1.0 + raised[6])
                source = pr[:, pl.ds(pl.multiple_of(at * BS, BS), BS)].astype(f32)
                scaled = source.reshape(8, 8, BS) * weight[None]
                terms[i, pl.ds(e * L, L), pl.ds(k * BS, BS)] = scaled.reshape(L, BS).astype(bf16)
            for r in range(BS // 16):
                halves = []
                for h in range(2):
                    base = columns[i][r * 16 + h * 8 : r * 16 + h * 8 + 8, :] - energies[e]
                    left = powers(base)[:6]
                    products = []
                    for k in range(KB):
                        product = left[0] + rows[k][0]
                        for j in range(1, 6):
                            product = product * (left[j] + rows[k][j])
                        products.append(product)
                    halves.append(products)
                for k in range(KB):
                    coupling = bl[i, pl.ds(r * 16, 16), pl.ds(k * BS, BS)].astype(f32)
                    product = jnp.concatenate([halves[0][k], halves[1][k]], 0)
                    mix[i, e, pl.ds(r * 16, 16), pl.ds(k * BS, BS)] = (coupling * product).astype(bf16)

        coupled = dot_nt(terms[i], bl[i])
        near = jnp.broadcast_to(onsite[pl.ds(i, 1), :], (8, BS))
        source = pr[:, pl.ds(i * BS, BS)].astype(f32).reshape(8, 8, BS)
        for e in range(local):
            mixed = dot_nt(terms[i, pl.ds(e * L, L), :], mix[i, e])
            shift = near - energies[e]
            weight = 1.0 / (1.0 + powers(shift)[6])
            first = weight[None] * (source - mixed.reshape(8, 8, BS))
            second = shift[None] * first + coupled[e * L : (e + 1) * L].reshape(8, 8, BS)
            kept = (
                lax.broadcasted_iota(jnp.int32, (8, 8, BS), 0) * 8
                + lax.broadcasted_iota(jnp.int32, (8, 8, BS), 1)
            ) < ranks[e]
            first = jnp.where(kept, first, 0.0).reshape(L, BS)
            second = jnp.where(kept, second, 0.0).reshape(L, BS)
            high, low = split(first)
            big[e, pl.ds(0, L), pl.ds(i * BS, BS)] = high
            big[e, pl.ds(L, L), pl.ds(i * BS, BS)] = low
            high, low = split(second)
            big[e, pl.ds(2 * L, L), pl.ds(i * BS, BS)] = high
            big[e, pl.ds(3 * L, L), pl.ds(i * BS, BS)] = low
            wide[e, i] = second

    states = []
    offset = lax.rem(position, BS // 8) * 8
    for e in range(local):
        sums = dot_nt(big[e, pl.ds(0, 2 * L), :], big[e])
        sums = (sums[:L] + sums[L:]) * (1.0 / NC)
        gram = sums[:, :BS] + pltpu.roll(sums[:, :BS], L, 1)
        cross = sums[:, BS:] + pltpu.roll(sums[:, BS:], L, 1)
        state = []
        for t in range(8):
            block = jnp.where(lane_index < L, gram[t * 8 : t * 8 + 8], cross[t * 8 : t * 8 + 8])
            state.append(jnp.where(lane_index == sub_index + t * 8, block + 1.0, block))
        mine = wide[e, lax.div(position, BS // 8)]
        mine = pltpu.roll(mine, lax.rem(BS - offset, BS), 1)
        mine = jnp.concatenate([mine, jnp.zeros((BS - L, BS), f32)], 0).T[:8]
        state.append(mine)
        states.append(state)

    for step in range(L):
        at, sub = divmod(step, 8)
        for e in range(local):
            state = states[e]
            row = state[at][sub : sub + 1, :]
            pivot = jnp.broadcast_to(row * (1.0 / row[:, step : step + 1]), (8, BS))
            for t in range(at, 9):
                state[t] = state[t] - state[t][:, step : step + 1] * pivot

    for e in range(local):
        reduced = jnp.where(lane_index < L, 0.0, states[e][8])
        reduced = reduced + pltpu.roll(reduced, L, 1)
        high, low = split(reduced)
        full = dot_nn(jnp.concatenate([high, low], 0), big[e, pl.ds(0, 2 * L), :])
        sigma = ((full[:8] + full[8:]) * (-1.0 / L)).astype(bf16)
        for peer in range(out.shape[0]):
            out[peer, e] = sigma


def place_kernel(incoming, owners, out):
    mine = lax.axis_index("energy")
    out[...] = jnp.zeros(out.shape, out.dtype)
    count = jnp.int32(0)
    for index in range(owners.shape[1]):
        hit = owners[0, index] == mine

        @pl.when(hit)
        def _():
            out[0, jnp.minimum(count, out.shape[1] - 1), 0] = incoming[index // 2, index % 2]

        count = count + hit.astype(jnp.int32)


def body(energies, onsite, blocks, pattern, probes, ranks, owner_map):
    local = energies.shape[0]
    groups = lax.axis_size("energy")
    rows = NC // lax.axis_size("contour")
    row_blocks = blocks.shape[0]
    smem = pl.BlockSpec(memory_space=pltpu.SMEM)
    vmem = pl.BlockSpec(memory_space=pltpu.VMEM)
    anywhere = pl.BlockSpec(memory_space=pl.ANY)
    arrays = (energies, ranks, onsite.reshape(row_blocks, BS), pattern.T, probes, blocks)
    sigma = pl.pallas_call(
        sigma_kernel,
        out_shape=pltpu.VMEM((groups, local, rows, NC), bf16),
        in_specs=[anywhere] * len(arrays),
        out_specs=vmem,
        scratch_shapes=[
            pltpu.SMEM(energies.shape, f32),
            pltpu.SMEM(ranks.shape, jnp.int32),
            pltpu.VMEM((row_blocks, BS), f32),
            pltpu.SMEM((KB, row_blocks), jnp.int32),
            pltpu.VMEM(probes.shape, bf16),
            pltpu.VMEM((NEAR, BS, KB * BS), bf16),
            pltpu.VMEM((NEAR, local, BS, KB * BS), bf16),
            pltpu.VMEM((NEAR, local * L, KB * BS), bf16),
            pltpu.VMEM((local, 4 * L, NC), bf16),
            pltpu.VMEM((local, NEAR, L, BS), f32),
            pltpu.SemaphoreType.DMA((5 + KB,)),
        ],
        compiler_params=pltpu.CompilerParams(vmem_limit_bytes=32 * 2**20),
        name="sigma",
    )(*(pltpu.with_memory_space_constraint(array, pltpu.HBM) for array in arrays))
    incoming = lax.all_to_all(sigma, "energy", 0, 0)
    return pl.pallas_call(
        place_kernel,
        out_shape=jax.ShapeDtypeStruct((1, local + 1, 2, rows, NC), bf16),
        in_specs=[vmem, smem],
        out_specs=vmem,
        name="place",
    )(incoming, owner_map.T)


def solution(mesh):
    placed = (P("energy"), P(), P(), P(), P(), P("energy"), P())
    return jax.shard_map(
        body,
        mesh=mesh,
        in_specs=placed,
        out_specs=P("energy", None, None, "contour", None),
        check_vma=False,
    )
```

```python
import jax
import jax.numpy as jnp
from jax import lax
from jax.experimental import pallas as pl
from jax.experimental.pallas import tpu as pltpu
from jax.sharding import PartitionSpec as P


L = 64
NC = 512
BS = 128
KB = 3
NEAR = NC // BS
f32 = jnp.float32
bf16 = jnp.bfloat16

def dot_nt(left, right):
    return lax.dot_general(left, right, (((1,), (1,)), ((), ())), preferred_element_type=f32)

def dot_nn(left, right):
    return lax.dot_general(left, right, (((1,), (0,)), ((), ())), preferred_element_type=f32)

def split(x):
    high = x.astype(bf16)
    return high, (x - high.astype(f32)).astype(bf16)

def spread_lane(x, lanes):
    return jnp.take_along_axis(x, lanes, axis=1)


def spread_row(x, row):
    return jnp.broadcast_to(x[row : row + 1, :], x.shape)


def powers(base):
    out = [base]
    for _ in range(6):
        out.append(out[-1] * out[-1])
    return out

def sigma_kernel(
    energies_in, ranks_in, onsite_in, pattern_in, owners_in, probes, blocks, out, slots,
    energies, ranks, onsite, pattern, owners, pr, bl, mix, near_terms, big, wide, bp, sems,
):
    local = energies.shape[0]
    small_copies = [
        pltpu.make_async_copy(source, target, sems.at[n])
        for n, (source, target) in enumerate(
            (
                (onsite_in, onsite),
                (pattern_in, pattern),
                (energies_in, energies),
                (ranks_in, ranks),
                (owners_in, owners),
            )
        )
    ]
    block_copies = [
        pltpu.make_async_copy(blocks.at[i], bl.at[i], sems.at[6 + i]) for i in range(NEAR)
    ]
    probe_copy = pltpu.make_async_copy(probes, pr, sems.at[5])
    for copy in small_copies + block_copies + [probe_copy]:
        copy.start()
    position = lax.axis_index("contour")
    sub_index = lax.broadcasted_iota(jnp.int32, (8, BS), 0)
    lane_index = lax.broadcasted_iota(jnp.int32, (8, BS), 1)

    for copy in small_copies:
        copy.wait()
    columns = []
    for i in range(NEAR):
        columns.append(jnp.broadcast_to(onsite[pl.ds(i, 1), :], (BS, BS)).T)

    for i in range(NEAR):
        block_copies[i].wait()
        for e in range(local):
            rows = []
            for k in range(KB):
                row = jnp.broadcast_to(onsite[pl.ds(pattern[k, i], 1), :], (8, BS)) - energies[e]
                raised = powers(row)
                rows.append((raised, 1.0 / (1.0 + raised[6])))
            for r in range(BS // 16):
                coupling = [bl[i, k, pl.ds(r * 16, 16), :].astype(f32) for k in range(KB)]
                scaled = [[None, None] for k in range(KB)]
                mixed = [[None, None] for k in range(KB)]
                for h in range(2):
                    left = powers(columns[i][r * 16 + h * 8 : r * 16 + h * 8 + 8, :] - energies[e])
                    for k in range(KB):
                        raised, weight = rows[k]
                        product = left[0] + raised[0]
                        for j in range(1, 6):
                            product = product * (left[j] + raised[j])
                        scaled[k][h] = coupling[k][h * 8 : h * 8 + 8] * weight
                        mixed[k][h] = scaled[k][h] * product
                for k in range(KB):
                    high, low = split(jnp.concatenate(mixed[k], 0))
                    plain = jnp.concatenate(scaled[k], 0).astype(bf16)
                    for n, part in enumerate((high, low, plain)):
                        mix[i, pl.ds((3 * e + n) * BS + r * 16, 16), pl.ds(k * BS, BS)] = part
    probe_copy.wait()

    for i in range(NEAR):
        for k in range(KB):
            near_terms[i, :, pl.ds(k * BS, BS)] = pr[:, pl.ds(pl.multiple_of(pattern[k, i] * BS, BS), BS)]
        coupled = dot_nt(near_terms[i], mix[i])
        near = jnp.broadcast_to(onsite[pl.ds(i, 1), :], (8, BS))
        source = pr[:, pl.ds(i * BS, BS)].astype(f32).reshape(8, 8, BS)
        for e in range(local):
            parts = [
                coupled[:, (3 * e + n) * BS : (3 * e + n + 1) * BS].reshape(8, 8, BS) for n in range(3)
            ]
            shift = near - energies[e]
            weight = 1.0 / (1.0 + powers(shift)[6])
            first = weight[None] * (source - (parts[0] + parts[1]))
            second = shift[None] * first + parts[2]
            kept = (
                lax.broadcasted_iota(jnp.int32, (8, 8, BS), 0) * 8
                + lax.broadcasted_iota(jnp.int32, (8, 8, BS), 1)
            ) < ranks[e]
            first = jnp.where(kept, first, 0.0).reshape(L, BS)
            second = jnp.where(kept, second, 0.0).reshape(L, BS)
            for n, part in enumerate(split(first) + split(second)):
                big[pl.ds((n * local + e) * L, L), pl.ds(i * BS, BS)] = part
            wide[i, pl.ds(e * L, L), :] = second

    offset = lax.rem(position, BS // 8) * 8
    sums = dot_nt(big[pl.ds(0, 2 * BS), :], big[...]) * (1.0 / NC)
    grams = []
    for e in range(local):
        high = sums[e * L : (e + 1) * L]
        low = sums[BS + e * L : BS + (e + 1) * L]
        grams.append(high[:, :BS] + (high[:, BS : 2 * BS] + low[:, :BS]))
        cross = high[:, 2 * BS : 3 * BS] + (high[:, 3 * BS :] + low[:, 2 * BS : 3 * BS])
        lanes = lax.broadcasted_iota(jnp.int32, (L, BS), 1)
        high, low = split(jnp.where(lanes // L == e, cross, 0.0))
        left = jnp.concatenate(
            [jnp.concatenate([high, high], 1), jnp.concatenate([low, jnp.zeros_like(low)], 1)], 0
        )
        applied = dot_nn(left, big[pl.ds(0, 2 * BS), :])
        high, low = split(applied[:L] + applied[L:])
        bp[pl.ds(e * L, L), :] = high
        bp[pl.ds((local + e) * L, L), :] = low
    state = []
    for t in range(L // 8):
        block = jnp.where(lane_index < L, grams[0][t * 8 : t * 8 + 8], grams[1][t * 8 : t * 8 + 8])
        state.append(jnp.where(lane_index % L == sub_index + t * 8, block + 1.0, block))
    mine = wide[lax.div(position, BS // 8)]
    mine = pltpu.roll(mine, lax.rem(BS - offset, BS), 1)
    state.append(mine.T[:8])
    half = (lane_index // L) * L

    unit = (lane_index % 8 == sub_index).astype(f32)
    inside = [spread_lane(state[0], half + n) for n in range(8)]
    for block in range(L // 8):
      last = block == L // 8 - 1
      column = half + block * 8
      factors = [
          [spread_lane(state[t], column + n) for n in range(8)] for t in range(block + 1, 9)
      ]
      ahead = [] if last else [spread_lane(state[block], column + 8 + n) for n in range(8)]
      following = [] if last else [spread_lane(state[block + 1], column + 8 + n) for n in range(8)]
      within = lane_index % L // 8 == block
      rows = jnp.where(within, unit, state[block])
      inverses = []
      for n in range(8):
          inverse = 1.0 / spread_row(inside[n], n)
          inverses.append(inverse)
          for m in range(n + 1, 8):
              scaled = spread_row(inside[m], n) * inverse
              inside[m] = jnp.where(sub_index == n, scaled, inside[m] - inside[n] * scaled)
      for n in range(8):
          for m in range(len(ahead)):
              scaled = spread_row(ahead[m], n) * inverses[n]
              ahead[m] = jnp.where(sub_index == n, scaled, ahead[m] - inside[n] * scaled)
          pivot = spread_row(rows, n) * inverses[n]
          rows = jnp.where(sub_index == n, pivot, rows - inside[n] * pivot)
      inside = []
      for m in range(len(ahead)):
          total = following[m]
          for n in range(8):
              total = total - factors[0][n] * spread_row(ahead[m], n)
          inside.append(total)
      solved = [spread_row(rows, n) for n in range(8)]
      for t in range(block + 1, 9):
          kept = jnp.where(within, 0.0, state[t])
          for n in range(8):
              kept = kept - factors[t - block - 1][n] * solved[n]
          state[t] = kept

    mine = lax.axis_index("energy")
    chosen = [jnp.int32(-1) for _ in range(slots.shape[0])]
    count = jnp.int32(0)
    for index in range(owners.shape[1]):
        hit = owners[0, index] == mine
        for c in range(len(chosen)):
            chosen[c] = jnp.where(hit & (count == c), index, chosen[c])
        count = count + hit.astype(jnp.int32)
    for c in range(len(chosen)):
        slots[c] = jnp.full(slots.shape[1:], chosen[c], jnp.int32)

    reduced = state[8]
    parts = []
    for e in range(local):
        high, low = split(jnp.where(half == e * L, reduced, 0.0))
        parts.append(jnp.concatenate([high, high], 1))
        parts.append(jnp.concatenate([low, jnp.zeros_like(low)], 1))
    full = dot_nn(jnp.concatenate(parts, 0), bp[...])
    for e in range(local):
        sigma = ((full[16 * e : 16 * e + 8] + full[16 * e + 8 : 16 * e + 16]) * (-1.0 / L)).astype(bf16)
        for peer in range(out.shape[0]):
            out[peer, e] = sigma

def place_kernel(incoming, slots, out):
    groups, local, rows, columns = incoming.shape
    zeros = jnp.zeros((rows, columns), out.dtype)
    sources = [incoming[n // local, n % local].astype(f32) for n in range(groups * local)]
    for c in range(out.shape[1]):
        index = jnp.concatenate([slots[c]] * (columns // BS), 1)
        total = jnp.zeros((rows, columns), f32)
        for n, source in enumerate(sources):
            total = jnp.where(index == n, source, total)
        out[0, c, 0] = total.astype(out.dtype)
        out[0, c, 1] = zeros


def body(energies, onsite, blocks, pattern, probes, ranks, owner_map):
    local = energies.shape[0]
    groups = lax.axis_size("energy")
    rows = NC // lax.axis_size("contour")
    row_blocks = blocks.shape[0]
    vmem = pl.BlockSpec(memory_space=pltpu.VMEM)
    anywhere = pl.BlockSpec(memory_space=pl.ANY)
    arrays = (
        energies, ranks, onsite.reshape(row_blocks, BS), pattern.T, owner_map.T, probes, blocks
    )
    sigma, slots = pl.pallas_call(
        sigma_kernel,
        out_shape=(
            pltpu.VMEM((groups, local, rows, NC), bf16),
            pltpu.VMEM((local + 1, rows, BS), jnp.int32),
        ),
        in_specs=[anywhere] * len(arrays),
        out_specs=(vmem, vmem),
        scratch_shapes=[
            pltpu.SMEM(energies.shape, f32),
            pltpu.SMEM(ranks.shape, jnp.int32),
            pltpu.VMEM((row_blocks, BS), f32),
            pltpu.SMEM((KB, row_blocks), jnp.int32),
            pltpu.SMEM((1, owner_map.shape[0]), jnp.int32),
            pltpu.VMEM(probes.shape, bf16),
            pltpu.VMEM((NEAR, KB, BS, BS), bf16),
            pltpu.VMEM((NEAR, 3 * local * BS, KB * BS), bf16),
            pltpu.VMEM((NEAR, L, KB * BS), bf16),
            pltpu.VMEM((4 * local * L, NC), bf16),
            pltpu.VMEM((NEAR, local * L, BS), f32),
            pltpu.VMEM((2 * local * L, NC), bf16),
            pltpu.SemaphoreType.DMA((6 + NEAR,)),
        ],
        compiler_params=pltpu.CompilerParams(vmem_limit_bytes=32 * 2**20),
        name="sigma",
    )(*(pltpu.with_memory_space_constraint(array, pltpu.HBM) for array in arrays))
    incoming = lax.all_to_all(sigma, "energy", 0, 0)
    return pl.pallas_call(
        place_kernel,
        out_shape=jax.ShapeDtypeStruct((1, local + 1, 2, rows, NC), bf16),
        in_specs=[vmem, vmem],
        out_specs=vmem,
        name="place",
    )(
        pltpu.with_memory_space_constraint(incoming, pltpu.VMEM),
        pltpu.with_memory_space_constraint(slots, pltpu.VMEM),
    )


def solution(mesh):
    placed = (P("energy"), P(), P(), P(), P(), P("energy"), P())
    return jax.shard_map(
        body,
        mesh=mesh,
        in_specs=placed,
        out_specs=P("energy", None, None, "contour", None),
        check_vma=False,
    )
```

```python
import jax
import jax.numpy as jnp
from jax import lax
from jax.experimental import pallas as pl
from jax.experimental.pallas import tpu as pltpu
from jax.sharding import PartitionSpec as P


L = 64
NC = 512
BS = 128
KB = 3
NEAR = NC // BS
f32 = jnp.float32
bf16 = jnp.bfloat16

def dot_nt(left, right):
    return lax.dot_general(left, right, (((1,), (1,)), ((), ())), preferred_element_type=f32)

def dot_nn(left, right):
    return lax.dot_general(left, right, (((1,), (0,)), ((), ())), preferred_element_type=f32)

def dot_tn(left, right):
    return lax.dot_general(left, right, (((0,), (0,)), ((), ())), preferred_element_type=f32)


def split(x):
    high = x.astype(bf16)
    return high, (x - high.astype(f32)).astype(bf16)

def spread_lane(x, lanes):
    return jnp.take_along_axis(x, lanes, axis=1)


def spread_row(x, row, rows=8):
    return jnp.broadcast_to(x[row : row + 1, :], (rows, x.shape[1]))


def split_wide(x):
    high = x.astype(bf16).astype(f32)
    return high, x - high


def ladder(x, exponent):
    square = x * x
    fourth = square * square
    out = jnp.where(exponent % 2 == 1, x, 1.0)
    out = jnp.where(exponent // 2 % 2 == 1, out * square, out)
    out = jnp.where(exponent // 4 == 1, out * fourth, out)
    return out, fourth * fourth


def powers(base):
    out = [base]
    for _ in range(6):
        out.append(out[-1] * out[-1])
    return out

def sigma_kernel(
    energies_in, ranks_in, onsite_in, pattern_in, owners_in, probes, blocks, out, slots,
    energies, ranks, onsite, pattern, owners, pr, bl, mix, near_terms, big, bp,
    left_rows, right_rows, products, sems,
):
    local = energies.shape[0]
    small_copies = [
        pltpu.make_async_copy(source, target, sems.at[n])
        for n, (source, target) in enumerate(
            (
                (onsite_in, onsite),
                (pattern_in, pattern),
                (energies_in, energies),
                (ranks_in, ranks),
                (owners_in, owners),
            )
        )
    ]
    block_copies = [
        pltpu.make_async_copy(
            blocks.at[pl.ds(0, NEAR), k], bl.at[:, :, pl.ds(k * BS, BS)], sems.at[6 + k]
        )
        for k in range(KB)
    ]
    probe_copy = pltpu.make_async_copy(probes, pr, sems.at[5])
    for copy in small_copies + block_copies + [probe_copy]:
        copy.start()
    position = lax.axis_index("contour")
    sub_index = lax.broadcasted_iota(jnp.int32, (8, BS), 0)
    lane_index = lax.broadcasted_iota(jnp.int32, (8, BS), 1)

    for copy in small_copies:
        copy.wait()
    all_weights = []
    for i in range(NEAR):
        near = spread_row(onsite[pl.ds(i, 1), :], 0, 8)
        for e in range(local):
            low_order, raised = ladder(near - energies[e], sub_index)
            high_order, _ = ladder(raised, sub_index)
            for h, table in enumerate((low_order, high_order)):
                high, low = split_wide(table)
                at = i * BS + (e * 2 + h) * 32
                left_rows[pl.ds(at, 32), :] = jnp.concatenate([high, high, low, low], 0).astype(bf16)
    for i in range(NEAR):
        weights = []
        for k in range(KB):
            far = spread_row(onsite[pl.ds(pattern[k, i], 1), :], 0, 8)
            for e in range(local):
                low_order, raised = ladder(far - energies[e], 7 - sub_index)
                high_order, last = ladder(raised, 7 - sub_index)
                weight = 1.0 / (1.0 + last)
                weights.append(weight)
                for h, table in enumerate((low_order, high_order * weight)):
                    high, low = split_wide(table)
                    right_rows[i, pl.ds((e * 2 + h) * 32, 32), pl.ds(k * BS, BS)] = jnp.concatenate(
                        [high, low, high, low], 0
                    ).astype(bf16)
        for g in range(2 * local):
            products[i, pl.ds(g * BS, BS), :] = dot_tn(
                left_rows[pl.ds(i * BS + g * 32, 32), :], right_rows[i, pl.ds(g * 32, 32), :]
            )
        all_weights.append(weights)
    for copy in block_copies:
        copy.wait()

    def mix_block(i):
        for k in range(KB):
            for r in range(BS // 16):
                coupling = bl[i, pl.ds(r * 16, 16), pl.ds(k * BS, BS)].astype(f32)
                for e in range(local):
                    low_order = products[i, pl.ds(e * 2 * BS + r * 16, 16), pl.ds(k * BS, BS)]
                    high_order = products[i, pl.ds((e * 2 + 1) * BS + r * 16, 16), pl.ds(k * BS, BS)]
                    high, low = split(coupling * (low_order * high_order))
                    for n, part in enumerate((high, low)):
                        mix[i, pl.ds((2 * e + n) * BS + r * 16, 16), pl.ds(k * BS, BS)] = part

    def gather_terms(i):
        for k in range(KB):
            far = pr[:, pl.ds(pl.multiple_of(pattern[k, i] * BS, BS), BS)]
            near_terms[i, pl.ds(0, L), pl.ds(k * BS, BS)] = far
            far = far.astype(f32).reshape(8, 8, BS)
            for e in range(local):
                scaled = far * all_weights[i][k * local + e][None]
                near_terms[i, pl.ds((1 + e) * L, L), pl.ds(k * BS, BS)] = scaled.reshape(L, BS).astype(bf16)

    def couple(i):
        return (
            dot_nt(near_terms[i, pl.ds(0, L), :], mix[i]),
            dot_nt(near_terms[i, pl.ds(L, local * L), :], bl[i]),
        )

    def finish(i, coupled, plain):
        near = jnp.broadcast_to(onsite[pl.ds(i, 1), :], (8, BS))
        source = pr[:, pl.ds(i * BS, BS)].astype(f32).reshape(8, 8, BS)
        for e in range(local):
            parts = [
                coupled[:, (2 * e + n) * BS : (2 * e + n + 1) * BS].reshape(8, 8, BS) for n in range(2)
            ]
            shift = near - energies[e]
            weight = 1.0 / (1.0 + powers(shift)[6])
            first = weight[None] * (source - (parts[0] + parts[1]))
            second = shift[None] * first + plain[e * L : (e + 1) * L].reshape(8, 8, BS)
            kept = (
                lax.broadcasted_iota(jnp.int32, (8, 8, BS), 0) * 8
                + lax.broadcasted_iota(jnp.int32, (8, 8, BS), 1)
            ) < ranks[e]
            first = jnp.where(kept, first, 0.0).reshape(L, BS)
            second = jnp.where(kept, second, 0.0).reshape(L, BS)
            for n, part in enumerate(split(first) + split(second)):
                big[pl.ds((n * local + e) * L, L), pl.ds(i * BS, BS)] = part

    probe_copy.wait()
    pending = None
    for i in range(NEAR):
        mix_block(i)
        gather_terms(i)
        done = couple(i)
        if pending is not None:
            finish(i - 1, *pending)
        pending = done
    finish(NEAR - 1, *pending)


    offset = lax.rem(position, BS // 8) * 8
    sums = dot_nt(big[pl.ds(0, 2 * BS), :], big[...]) * (1.0 / NC)
    grams = []
    for e in range(local):
        high = sums[e * L : (e + 1) * L]
        low = sums[BS + e * L : BS + (e + 1) * L]
        grams.append(high[:, :BS] + (high[:, BS : 2 * BS] + low[:, :BS]))
        cross = high[:, 2 * BS : 3 * BS] + (high[:, 3 * BS :] + low[:, 2 * BS : 3 * BS])
        lanes = lax.broadcasted_iota(jnp.int32, (L, BS), 1)
        high, low = split(jnp.where(lanes // L == e, cross, 0.0))
        left = jnp.concatenate(
            [jnp.concatenate([high, high], 1), jnp.concatenate([low, jnp.zeros_like(low)], 1)], 0
        )
        applied = dot_nn(left, big[pl.ds(0, 2 * BS), :])
        high, low = split(applied[:L] + applied[L:])
        bp[pl.ds(e * L, L), :] = high
        bp[pl.ds((local + e) * L, L), :] = low
    state = []
    for t in range(L // 8):
        block = jnp.where(lane_index < L, grams[0][t * 8 : t * 8 + 8], grams[1][t * 8 : t * 8 + 8])
        state.append(jnp.where(lane_index % L == sub_index + t * 8, block + 1.0, block))
    rows = lax.broadcasted_iota(jnp.int32, (16, BS), 0)
    pick = (lax.broadcasted_iota(jnp.int32, (16, BS), 1) == rows + offset).astype(bf16)
    near_block = pl.multiple_of(lax.div(position, BS // 8) * BS, BS)
    mine = dot_nt(pick, big[pl.ds(2 * BS, 2 * BS), pl.ds(near_block, BS)])[:8]
    state.append(mine[:, :BS] + mine[:, BS:])
    half = (lane_index // L) * L

    unit = (lane_index % 8 == sub_index).astype(f32)
    inside = [spread_lane(state[0], half + n) for n in range(8)]
    for block in range(L // 8):
      last = block == L // 8 - 1
      column = half + block * 8
      factors = [
          [spread_lane(state[t], column + n) for n in range(8)] for t in range(block + 1, 9)
      ]
      ahead = [] if last else [spread_lane(state[block], column + 8 + n) for n in range(8)]
      following = [] if last else [spread_lane(state[block + 1], column + 8 + n) for n in range(8)]
      within = lane_index % L // 8 == block
      rows = jnp.where(within, unit, state[block])
      inverses = []
      for n in range(8):
          inverse = 1.0 / spread_row(inside[n], n)
          inverses.append(inverse)
          for m in range(n + 1, 8):
              scaled = spread_row(inside[m], n) * inverse
              inside[m] = jnp.where(sub_index == n, scaled, inside[m] - inside[n] * scaled)
      for n in range(8):
          for m in range(len(ahead)):
              scaled = spread_row(ahead[m], n) * inverses[n]
              ahead[m] = jnp.where(sub_index == n, scaled, ahead[m] - inside[n] * scaled)
          pivot = spread_row(rows, n) * inverses[n]
          rows = jnp.where(sub_index == n, pivot, rows - inside[n] * pivot)
      inside = []
      for m in range(len(ahead)):
          total = following[m]
          for n in range(8):
              total = total - factors[0][n] * spread_row(ahead[m], n)
          inside.append(total)
      solved = [spread_row(rows, n) for n in range(8)]
      for t in range(block + 1, 9):
          kept = jnp.where(within, 0.0, state[t])
          for n in range(8):
              kept = kept - factors[t - block - 1][n] * solved[n]
          state[t] = kept

    mine = lax.axis_index("energy")
    chosen = [jnp.int32(-1) for _ in range(slots.shape[0])]
    count = jnp.int32(0)
    for index in range(owners.shape[1]):
        hit = owners[0, index] == mine
        for c in range(len(chosen)):
            chosen[c] = jnp.where(hit & (count == c), index, chosen[c])
        count = count + hit.astype(jnp.int32)
    for c in range(len(chosen)):
        slots[c] = jnp.full(slots.shape[1:], chosen[c], jnp.int32)

    reduced = state[8]
    parts = []
    for e in range(local):
        high, low = split(jnp.where(half == e * L, reduced, 0.0))
        parts.append(jnp.concatenate([high, high], 1))
        parts.append(jnp.concatenate([low, jnp.zeros_like(low)], 1))
    full = dot_nn(jnp.concatenate(parts, 0), bp[...])
    for e in range(local):
        sigma = ((full[16 * e : 16 * e + 8] + full[16 * e + 8 : 16 * e + 16]) * (-1.0 / L)).astype(bf16)
        for peer in range(out.shape[0]):
            out[peer, e] = sigma

def place_kernel(incoming, slots, out):
    groups, local, rows, columns = incoming.shape
    zeros = jnp.zeros((rows, columns), out.dtype)
    sources = [incoming[n // local, n % local].astype(f32) for n in range(groups * local)]
    for c in range(out.shape[1]):
        index = jnp.concatenate([slots[c]] * (columns // BS), 1)
        total = jnp.zeros((rows, columns), f32)
        for n, source in enumerate(sources):
            total = jnp.where(index == n, source, total)
        out[0, c, 0] = total.astype(out.dtype)
        out[0, c, 1] = zeros


def body(energies, onsite, blocks, pattern, probes, ranks, owner_map):
    local = energies.shape[0]
    groups = lax.axis_size("energy")
    rows = NC // lax.axis_size("contour")
    row_blocks = blocks.shape[0]
    vmem = pl.BlockSpec(memory_space=pltpu.VMEM)
    anywhere = pl.BlockSpec(memory_space=pl.ANY)
    arrays = (
        energies, ranks, onsite.reshape(row_blocks, BS), pattern.T, owner_map.T, probes, blocks
    )
    sigma, slots = pl.pallas_call(
        sigma_kernel,
        out_shape=(
            pltpu.VMEM((groups, local, rows, NC), bf16),
            pltpu.VMEM((local + 1, rows, BS), jnp.int32),
        ),
        in_specs=[anywhere] * len(arrays),
        out_specs=(vmem, vmem),
        scratch_shapes=[
            pltpu.SMEM(energies.shape, f32),
            pltpu.SMEM(ranks.shape, jnp.int32),
            pltpu.VMEM((row_blocks, BS), f32),
            pltpu.SMEM((KB, row_blocks), jnp.int32),
            pltpu.SMEM((1, owner_map.shape[0]), jnp.int32),
            pltpu.VMEM(probes.shape, bf16),
            pltpu.VMEM((NEAR, BS, KB * BS), bf16),
            pltpu.VMEM((NEAR, 2 * local * BS, KB * BS), bf16),
            pltpu.VMEM((NEAR, (1 + local) * L, KB * BS), bf16),
            pltpu.VMEM((4 * local * L, NC), bf16),
            pltpu.VMEM((2 * local * L, NC), bf16),
            pltpu.VMEM((NEAR * BS, BS), bf16),
            pltpu.VMEM((NEAR, BS, KB * BS), bf16),
            pltpu.VMEM((NEAR, 4 * BS, KB * BS), f32),
            pltpu.SemaphoreType.DMA((6 + NEAR,)),
        ],
        compiler_params=pltpu.CompilerParams(vmem_limit_bytes=32 * 2**20),
        name="sigma",
    )(*(pltpu.with_memory_space_constraint(array, pltpu.HBM) for array in arrays))
    incoming = lax.all_to_all(sigma, "energy", 0, 0)
    return pl.pallas_call(
        place_kernel,
        out_shape=jax.ShapeDtypeStruct((1, local + 1, 2, rows, NC), bf16),
        in_specs=[vmem, vmem],
        out_specs=vmem,
        name="place",
    )(
        pltpu.with_memory_space_constraint(incoming, pltpu.VMEM),
        pltpu.with_memory_space_constraint(slots, pltpu.VMEM),
    )


def solution(mesh):
    placed = (P("energy"), P(), P(), P(), P(), P("energy"), P())
    return jax.shard_map(
        body,
        mesh=mesh,
        in_specs=placed,
        out_specs=P("energy", None, None, "contour", None),
        check_vma=False,
    )
```

```python
import jax
import jax.numpy as jnp
from jax import lax
from jax.experimental import pallas as pl
from jax.experimental.pallas import tpu as pltpu
from jax.sharding import PartitionSpec as P


L = 64
NC = 512
BS = 128
KB = 3
NEAR = NC // BS
f32 = jnp.float32
bf16 = jnp.bfloat16

def dot_nt(left, right):
    return lax.dot_general(left, right, (((1,), (1,)), ((), ())), preferred_element_type=f32)

def dot_nn(left, right):
    return lax.dot_general(left, right, (((1,), (0,)), ((), ())), preferred_element_type=f32)

def dot_tn(left, right):
    return lax.dot_general(left, right, (((0,), (0,)), ((), ())), preferred_element_type=f32)


def split(x):
    high = x.astype(bf16)
    return high, (x - high.astype(f32)).astype(bf16)

def spread_lane(x, lanes):
    return jnp.take_along_axis(x, lanes, axis=1)


def spread_row(x, row, rows=8):
    return jnp.broadcast_to(x[row : row + 1, :], (rows, x.shape[1]))


def split_wide(x):
    high = x.astype(bf16).astype(f32)
    return high, x - high


def ladder(x, exponent):
    square = x * x
    fourth = square * square
    out = jnp.where(exponent % 2 == 1, x, 1.0)
    out = jnp.where(exponent // 2 % 2 == 1, out * square, out)
    out = jnp.where(exponent // 4 == 1, out * fourth, out)
    return out, fourth * fourth


def powers(base):
    out = [base]
    for _ in range(6):
        out.append(out[-1] * out[-1])
    return out

def sigma_kernel(
    energies_in, ranks_in, onsite_in, pattern_in, owners_in, probes, blocks, out, slots,
    energies, ranks, onsite, pattern, owners, pr, bl, mix, near_terms, big, bp,
    left_rows, right_rows, products, sems,
):
    local = energies.shape[0]
    small_copies = [
        pltpu.make_async_copy(source, target, sems.at[n])
        for n, (source, target) in enumerate(
            (
                (onsite_in, onsite),
                (pattern_in, pattern),
                (energies_in, energies),
                (ranks_in, ranks),
                (owners_in, owners),
            )
        )
    ]
    block_copies = [
        pltpu.make_async_copy(
            blocks.at[pl.ds(0, NEAR), k], bl.at[:, :, pl.ds(k * BS, BS)], sems.at[6 + k]
        )
        for k in range(KB)
    ]
    probe_copy = pltpu.make_async_copy(probes, pr, sems.at[5])
    for copy in small_copies + block_copies + [probe_copy]:
        copy.start()
    position = lax.axis_index("contour")
    sub_index = lax.broadcasted_iota(jnp.int32, (8, BS), 0)
    lane_index = lax.broadcasted_iota(jnp.int32, (8, BS), 1)

    for copy in small_copies:
        copy.wait()
    all_weights = []
    for i in range(NEAR):
        near = spread_row(onsite[pl.ds(i, 1), :], 0, 8)
        for e in range(local):
            low_order, raised = ladder(near - energies[e], sub_index)
            high_order, _ = ladder(raised, sub_index)
            for h, table in enumerate((low_order, high_order)):
                high, low = split_wide(table)
                at = i * BS + (e * 2 + h) * 32
                left_rows[pl.ds(at, 32), :] = jnp.concatenate([high, high, low, low], 0).astype(bf16)
    def power_block(i):
        weights = []
        for k in range(KB):
            far = spread_row(onsite[pl.ds(pattern[k, i], 1), :], 0, 8)
            for e in range(local):
                low_order, raised = ladder(far - energies[e], 7 - sub_index)
                high_order, last = ladder(raised, 7 - sub_index)
                weight = 1.0 / (1.0 + last)
                weights.append(weight)
                for h, table in enumerate((low_order, high_order * weight)):
                    high, low = split_wide(table)
                    right_rows[i, pl.ds((e * 2 + h) * 32, 32), pl.ds(k * BS, BS)] = jnp.concatenate(
                        [high, low, high, low], 0
                    ).astype(bf16)
        for g in range(2 * local):
            products[i, pl.ds(g * BS, BS), :] = dot_tn(
                left_rows[pl.ds(i * BS + g * 32, 32), :], right_rows[i, pl.ds(g * 32, 32), :]
            )
        all_weights.append(weights)
    for i in range(NEAR):
        power_block(i)
    for copy in block_copies:
        copy.wait()
    def mix_block(i):
        for k in range(KB):
            for r in range(BS // 16):
                coupling = bl[i, pl.ds(r * 16, 16), pl.ds(k * BS, BS)].astype(f32)
                for e in range(local):
                    low_order = products[i, pl.ds(e * 2 * BS + r * 16, 16), pl.ds(k * BS, BS)]
                    high_order = products[i, pl.ds((e * 2 + 1) * BS + r * 16, 16), pl.ds(k * BS, BS)]
                    high, low = split(coupling * (low_order * high_order))
                    for n, part in enumerate((high, low)):
                        mix[i, pl.ds((2 * e + n) * BS + r * 16, 16), pl.ds(k * BS, BS)] = part

    def gather_terms(i):
        for k in range(KB):
            far = pr[:, pl.ds(pl.multiple_of(pattern[k, i] * BS, BS), BS)]
            near_terms[i, pl.ds(0, L), pl.ds(k * BS, BS)] = far
            far = far.astype(f32).reshape(8, 8, BS)
            for e in range(local):
                scaled = far * all_weights[i][k * local + e][None]
                near_terms[i, pl.ds((1 + e) * L, L), pl.ds(k * BS, BS)] = scaled.reshape(L, BS).astype(bf16)

    def couple(i):
        return (
            dot_nt(near_terms[i, pl.ds(0, L), :], mix[i]),
            dot_nt(near_terms[i, pl.ds(L, local * L), :], bl[i]),
        )

    def finish(i, coupled, plain):
        near = jnp.broadcast_to(onsite[pl.ds(i, 1), :], (8, BS))
        source = pr[:, pl.ds(i * BS, BS)].astype(f32).reshape(8, 8, BS)
        for e in range(local):
            parts = [
                coupled[:, (2 * e + n) * BS : (2 * e + n + 1) * BS].reshape(8, 8, BS) for n in range(2)
            ]
            shift = near - energies[e]
            weight = 1.0 / (1.0 + powers(shift)[6])
            first = weight[None] * (source - (parts[0] + parts[1]))
            second = shift[None] * first + plain[e * L : (e + 1) * L].reshape(8, 8, BS)
            kept = (
                lax.broadcasted_iota(jnp.int32, (8, 8, BS), 0) * 8
                + lax.broadcasted_iota(jnp.int32, (8, 8, BS), 1)
            ) < ranks[e]
            first = jnp.where(kept, first, 0.0).reshape(L, BS)
            second = jnp.where(kept, second, 0.0).reshape(L, BS)
            for n, part in enumerate(split(first) + split(second)):
                big[pl.ds((n * local + e) * L, L), pl.ds(i * BS, BS)] = part

    probe_copy.wait()
    pending = None
    for i in range(NEAR):
        mix_block(i)
        gather_terms(i)
        done = couple(i)
        if pending is not None:
            finish(i - 1, *pending)
        pending = done
    finish(NEAR - 1, *pending)

    offset = lax.rem(position, BS // 8) * 8
    near_high, near_low = big[pl.ds(0, BS), :], big[pl.ds(BS, BS), :]
    wide = dot_nt(near_high, big[pl.ds(0, 2 * BS), :])
    square = (wide[:, :BS] + (wide[:, BS:] + dot_nt(near_low, near_high))) * (1.0 / NC)
    far = dot_nt(big[pl.ds(0, 2 * BS), :], big[pl.ds(2 * BS, BS), :])
    across = (far[:BS] + (far[BS:] + dot_nt(near_high, big[pl.ds(3 * BS, BS), :]))) * (1.0 / NC)
    grams = []
    for e in range(local):
        grams.append(square[e * L : (e + 1) * L])
        cross = across[e * L : (e + 1) * L]
        lanes = lax.broadcasted_iota(jnp.int32, (L, BS), 1)
        high, low = split(jnp.where(lanes // L == e, cross, 0.0))
        left = jnp.concatenate(
            [jnp.concatenate([high, high], 1), jnp.concatenate([low, jnp.zeros_like(low)], 1)], 0
        )
        applied = dot_nn(left, big[pl.ds(0, 2 * BS), :])
        high, low = split(applied[:L] + applied[L:])
        bp[pl.ds(e * L, L), :] = high
        bp[pl.ds((local + e) * L, L), :] = low
    state = []
    for t in range(L // 8):
        block = jnp.where(lane_index < L, grams[0][t * 8 : t * 8 + 8], grams[1][t * 8 : t * 8 + 8])
        state.append(jnp.where(lane_index % L == sub_index + t * 8, block + 1.0, block))
    rows = lax.broadcasted_iota(jnp.int32, (16, BS), 0)
    pick = (lax.broadcasted_iota(jnp.int32, (16, BS), 1) == rows + offset).astype(bf16)
    near_block = pl.multiple_of(lax.div(position, BS // 8) * BS, BS)
    mine = dot_nt(pick, big[pl.ds(2 * BS, 2 * BS), pl.ds(near_block, BS)])[:8]
    state.append(mine[:, :BS] + mine[:, BS:])
    half = (lane_index // L) * L

    unit = (lane_index % 8 == sub_index).astype(f32)
    inside = [spread_lane(state[0], half + n) for n in range(8)]
    for block in range(L // 8):
        column = half + block * 8
        factors = [
            [spread_lane(state[t], column + n) for n in range(8)] for t in range(block + 1, 9)
        ]
        beside = list(factors[0])
        following = [spread_lane(state[block + 1], column + 8 + n) for n in range(8)] if block < 7 else []
        within = lane_index % L // 8 == block
        rows = jnp.where(within, unit, state[block])
        for n in range(0, 8, 2):
            first, cross, second = (
                spread_row(inside[n], n), spread_row(inside[n], n + 1), spread_row(inside[n + 1], n + 1)
            )
            inverse = 1.0 / (first * second - cross * cross)
            first, cross, second = first * inverse, cross * inverse, second * inverse

            def solve(x, y):
                return second * x - cross * y, first * y - cross * x

            for m in range(n + 2, 8):
                x, y = solve(spread_row(inside[m], n), spread_row(inside[m], n + 1))
                left = inside[m] - (inside[n] * x + inside[n + 1] * y)
                inside[m] = jnp.where(sub_index == n, x, jnp.where(sub_index == n + 1, y, left))
                beside[m] = beside[m] - (beside[n] * x + beside[n + 1] * y)
            upper, lower = solve(beside[n], beside[n + 1])
            for m in range(len(following)):
                following[m] = following[m] - (
                    upper * spread_row(beside[n], m) + lower * spread_row(beside[n + 1], m)
                )
            x, y = solve(spread_row(rows, n), spread_row(rows, n + 1))
            left = rows - (inside[n] * x + inside[n + 1] * y)
            rows = jnp.where(sub_index == n, x, jnp.where(sub_index == n + 1, y, left))
        inside = following
        solved = [spread_row(rows, n) for n in range(8)]
        for t in range(block + 1, 9):
            kept = jnp.where(within, 0.0, state[t])
            for n in range(8):
                kept = kept - factors[t - block - 1][n] * solved[n]
            state[t] = kept

    mine = lax.axis_index("energy")
    chosen = [jnp.int32(-1) for _ in range(slots.shape[0])]
    count = jnp.int32(0)
    for index in range(owners.shape[1]):
        hit = owners[0, index] == mine
        for c in range(len(chosen)):
            chosen[c] = jnp.where(hit & (count == c), index, chosen[c])
        count = count + hit.astype(jnp.int32)
    for c in range(len(chosen)):
        slots[c] = jnp.full(slots.shape[1:], chosen[c], jnp.int32)

    reduced = state[8]
    parts = []
    for e in range(local):
        high, low = split(jnp.where(half == e * L, reduced, 0.0))
        parts.append(jnp.concatenate([high, high], 1))
        parts.append(jnp.concatenate([low, jnp.zeros_like(low)], 1))
    full = dot_nn(jnp.concatenate(parts, 0), bp[...])
    for e in range(local):
        sigma = ((full[16 * e : 16 * e + 8] + full[16 * e + 8 : 16 * e + 16]) * (-1.0 / L)).astype(bf16)
        for peer in range(out.shape[0]):
            out[peer, e] = sigma

def place_kernel(incoming, slots, out):
    groups, local, rows, columns = incoming.shape
    zeros = jnp.zeros((rows, columns), out.dtype)
    sources = [incoming[n // local, n % local].astype(f32) for n in range(groups * local)]
    for c in range(out.shape[1]):
        index = jnp.concatenate([slots[c]] * (columns // BS), 1)
        total = jnp.zeros((rows, columns), f32)
        for n, source in enumerate(sources):
            total = jnp.where(index == n, source, total)
        out[0, c, 0] = total.astype(out.dtype)
        out[0, c, 1] = zeros


def body(energies, onsite, blocks, pattern, probes, ranks, owner_map):
    local = energies.shape[0]
    groups = lax.axis_size("energy")
    rows = NC // lax.axis_size("contour")
    row_blocks = blocks.shape[0]
    vmem = pl.BlockSpec(memory_space=pltpu.VMEM)
    anywhere = pl.BlockSpec(memory_space=pl.ANY)
    arrays = (
        energies, ranks, onsite.reshape(row_blocks, BS), pattern.T, owner_map.T, probes, blocks
    )
    sigma, slots = pl.pallas_call(
        sigma_kernel,
        out_shape=(
            pltpu.VMEM((groups, local, rows, NC), bf16),
            pltpu.VMEM((local + 1, rows, BS), jnp.int32),
        ),
        in_specs=[anywhere] * len(arrays),
        out_specs=(vmem, vmem),
        scratch_shapes=[
            pltpu.SMEM(energies.shape, f32),
            pltpu.SMEM(ranks.shape, jnp.int32),
            pltpu.VMEM((row_blocks, BS), f32),
            pltpu.SMEM((KB, row_blocks), jnp.int32),
            pltpu.SMEM((1, owner_map.shape[0]), jnp.int32),
            pltpu.VMEM(probes.shape, bf16),
            pltpu.VMEM((NEAR, BS, KB * BS), bf16),
            pltpu.VMEM((NEAR, 2 * local * BS, KB * BS), bf16),
            pltpu.VMEM((NEAR, (1 + local) * L, KB * BS), bf16),
            pltpu.VMEM((4 * local * L, NC), bf16),
            pltpu.VMEM((2 * local * L, NC), bf16),
            pltpu.VMEM((NEAR * BS, BS), bf16),
            pltpu.VMEM((NEAR, BS, KB * BS), bf16),
            pltpu.VMEM((NEAR, 4 * BS, KB * BS), f32),
            pltpu.SemaphoreType.DMA((6 + NEAR,)),
        ],
        compiler_params=pltpu.CompilerParams(vmem_limit_bytes=32 * 2**20),
        name="sigma",
    )(*(pltpu.with_memory_space_constraint(array, pltpu.HBM) for array in arrays))
    incoming = lax.all_to_all(sigma, "energy", 0, 0)
    return pl.pallas_call(
        place_kernel,
        out_shape=jax.ShapeDtypeStruct((1, local + 1, 2, rows, NC), bf16),
        in_specs=[vmem, vmem],
        out_specs=vmem,
        name="place",
    )(
        pltpu.with_memory_space_constraint(incoming, pltpu.VMEM),
        pltpu.with_memory_space_constraint(slots, pltpu.VMEM),
    )


def solution(mesh):
    placed = (P("energy"), P(), P(), P(), P(), P("energy"), P())
    return jax.shard_map(
        body,
        mesh=mesh,
        in_specs=placed,
        out_specs=P("energy", None, None, "contour", None),
        check_vma=False,
    )
```

```python
import jax
import jax.numpy as jnp
from jax import lax
from jax.experimental import pallas as pl
from jax.experimental.pallas import tpu as pltpu
from jax.sharding import PartitionSpec as P


L = 64
NC = 512
BS = 128
KB = 3
CHAIN = (0, 2, 6)
NEAR = NC // BS
f32 = jnp.float32
bf16 = jnp.bfloat16

def follow(home, step, choose):
    out = home
    for n, at in enumerate(CHAIN):
        out = choose(home == at, CHAIN[(n + step) % len(CHAIN)], out)
    return out


def other_core(group, home):
    return group % 4 // 2 * ((home > 0))


def peer_positions(group, position, choose, groups):
    core = position % 2
    home = choose((group == 0) & (core == 0), follow(position - core, -1, choose), position - core)
    parity = (core + other_core(group, home)) % 2
    out = []
    for peer in range(groups):
        place = choose(parity == 0, follow(home, 1, choose), home) if peer == 0 else home
        out.append(place + (parity + other_core(peer, home)) % 2)
    return out


def exchange_groups(groups, positions):
    found = []
    for position in range(positions):
        at = peer_positions(0, position, lambda test, yes, no: yes if test else no, groups)
        found.append([group * positions + at[group] for group in range(groups)])
    return found


def dot_nt(left, right):
    return lax.dot_general(left, right, (((1,), (1,)), ((), ())), preferred_element_type=f32)

def dot_nn(left, right):
    return lax.dot_general(left, right, (((1,), (0,)), ((), ())), preferred_element_type=f32)

def dot_tn(left, right):
    return lax.dot_general(left, right, (((0,), (0,)), ((), ())), preferred_element_type=f32)


def split(x):
    high = x.astype(bf16)
    return high, (x - high.astype(f32)).astype(bf16)

def spread_lane(x, lanes):
    return jnp.take_along_axis(x, lanes, axis=1)


def spread_row(x, row, rows=8):
    return jnp.broadcast_to(x[row : row + 1, :], (rows, x.shape[1]))


def split_wide(x):
    high = x.astype(bf16).astype(f32)
    return high, x - high


def ladder(x, exponent):
    square = x * x
    fourth = square * square
    out = jnp.where(exponent % 2 == 1, x, 1.0)
    out = jnp.where(exponent // 2 % 2 == 1, out * square, out)
    out = jnp.where(exponent // 4 == 1, out * fourth, out)
    return out, fourth * fourth


def powers(base):
    out = [base]
    for _ in range(6):
        out.append(out[-1] * out[-1])
    return out

def sigma_kernel(
    energies_in, ranks_in, onsite_in, pattern_in, owners_in, probes, blocks, out, slots,
    energies, ranks, onsite, pattern, owners, pr, bl, mix, near_terms, big, bp,
    left_rows, right_rows, products, turned, ahead_rows, sems,
):
    local = energies.shape[0]
    small_copies = [
        pltpu.make_async_copy(source, target, sems.at[n])
        for n, (source, target) in enumerate(
            (
                (onsite_in, onsite),
                (pattern_in, pattern),
                (energies_in, energies),
                (ranks_in, ranks),
                (owners_in, owners),
            )
        )
    ]
    block_copies = [
        pltpu.make_async_copy(
            blocks.at[pl.ds(0, NEAR), k], bl.at[:, :, pl.ds(k * BS, BS)], sems.at[6 + k]
        )
        for k in range(KB)
    ]
    probe_copy = pltpu.make_async_copy(probes, pr, sems.at[5])
    for copy in small_copies + block_copies + [probe_copy]:
        copy.start()
    position = lax.axis_index("contour")
    sub_index = lax.broadcasted_iota(jnp.int32, (8, BS), 0)
    lane_index = lax.broadcasted_iota(jnp.int32, (8, BS), 1)

    for copy in small_copies:
        copy.wait()
    all_weights = []
    for i in range(NEAR):
        near = spread_row(onsite[pl.ds(i, 1), :], 0, 8)
        for e in range(local):
            low_order, raised = ladder(near - energies[e], sub_index)
            high_order, _ = ladder(raised, sub_index)
            for h, table in enumerate((low_order, high_order)):
                high, low = split_wide(table)
                at = i * BS + (e * 2 + h) * 32
                left_rows[pl.ds(at, 32), :] = jnp.concatenate([high, high, low, low], 0).astype(bf16)
    def power_block(i):
        weights = []
        for k in range(KB):
            far = spread_row(onsite[pl.ds(pattern[k, i], 1), :], 0, 8)
            for e in range(local):
                low_order, raised = ladder(far - energies[e], 7 - sub_index)
                high_order, last = ladder(raised, 7 - sub_index)
                weight = 1.0 / (1.0 + last)
                weights.append(weight)
                for h, table in enumerate((low_order, high_order * weight)):
                    high, low = split_wide(table)
                    right_rows[i, pl.ds((e * 2 + h) * 32, 32), pl.ds(k * BS, BS)] = jnp.concatenate(
                        [high, low, high, low], 0
                    ).astype(bf16)
        for g in range(2 * local):
            products[i, pl.ds(g * BS, BS), :] = dot_tn(
                left_rows[pl.ds(i * BS + g * 32, 32), :], right_rows[i, pl.ds(g * 32, 32), :]
            )
        all_weights.append(weights)
    for i in range(NEAR):
        power_block(i)
    for copy in block_copies:
        copy.wait()
    def mix_block(i):
        for k in range(KB):
            for r in range(BS // 16):
                coupling = bl[i, pl.ds(r * 16, 16), pl.ds(k * BS, BS)].astype(f32)
                for e in range(local):
                    low_order = products[i, pl.ds(e * 2 * BS + r * 16, 16), pl.ds(k * BS, BS)]
                    high_order = products[i, pl.ds((e * 2 + 1) * BS + r * 16, 16), pl.ds(k * BS, BS)]
                    high, low = split(coupling * (low_order * high_order))
                    for n, part in enumerate((high, low)):
                        mix[i, pl.ds((2 * e + n) * BS + r * 16, 16), pl.ds(k * BS, BS)] = part

    def gather_terms(i):
        for k in range(KB):
            far = pr[:, pl.ds(pl.multiple_of(pattern[k, i] * BS, BS), BS)]
            near_terms[i, pl.ds(0, L), pl.ds(k * BS, BS)] = far
            far = far.astype(f32).reshape(8, 8, BS)
            for e in range(local):
                scaled = far * all_weights[i][k * local + e][None]
                near_terms[i, pl.ds((1 + e) * L, L), pl.ds(k * BS, BS)] = scaled.reshape(L, BS).astype(bf16)

    def couple(i):
        return (
            dot_nt(near_terms[i, pl.ds(0, L), :], mix[i]),
            dot_nt(near_terms[i, pl.ds(L, local * L), :], bl[i]),
        )

    def finish(i, coupled, plain):
        near = jnp.broadcast_to(onsite[pl.ds(i, 1), :], (8, BS))
        source = pr[:, pl.ds(i * BS, BS)].astype(f32).reshape(8, 8, BS)
        for e in range(local):
            parts = [
                coupled[:, (2 * e + n) * BS : (2 * e + n + 1) * BS].reshape(8, 8, BS) for n in range(2)
            ]
            shift = near - energies[e]
            weight = 1.0 / (1.0 + powers(shift)[6])
            first = weight[None] * (source - (parts[0] + parts[1]))
            second = shift[None] * first + plain[e * L : (e + 1) * L].reshape(8, 8, BS)
            kept = (
                lax.broadcasted_iota(jnp.int32, (8, 8, BS), 0) * 8
                + lax.broadcasted_iota(jnp.int32, (8, 8, BS), 1)
            ) < ranks[e]
            first = jnp.where(kept, first, 0.0).reshape(L, BS)
            second = jnp.where(kept, second, 0.0).reshape(L, BS)
            for n, part in enumerate(split(first) + split(second)):
                big[pl.ds((n * local + e) * L, L), pl.ds(i * BS, BS)] = part

    probe_copy.wait()
    pending = None
    for i in range(NEAR):
        mix_block(i)
        gather_terms(i)
        done = couple(i)
        if pending is not None:
            finish(i - 1, *pending)
        pending = done
    finish(NEAR - 1, *pending)

    near_high, near_low = big[pl.ds(0, BS), :], big[pl.ds(BS, BS), :]
    wide = dot_nt(near_high, big[pl.ds(0, 2 * BS), :])
    square = (wide[:, :BS] + (wide[:, BS:] + dot_nt(near_low, near_high))) * (1.0 / NC)
    far = dot_nt(big[pl.ds(0, 2 * BS), :], big[pl.ds(2 * BS, BS), :])
    across = (far[:BS] + (far[BS:] + dot_nt(near_high, big[pl.ds(3 * BS, BS), :]))) * (1.0 / NC)
    grams = []
    for e in range(local):
        grams.append(square[e * L : (e + 1) * L])
        cross = across[e * L : (e + 1) * L]
        lanes = lax.broadcasted_iota(jnp.int32, (L, BS), 1)
        high, low = split(jnp.where(lanes // L == e, cross, 0.0))
        left = jnp.concatenate(
            [jnp.concatenate([high, high], 1), jnp.concatenate([low, jnp.zeros_like(low)], 1)], 0
        )
        applied = dot_nn(left, big[pl.ds(0, 2 * BS), :])
        high, low = split(applied[:L] + applied[L:])
        bp[pl.ds(e * L, L), :] = high
        bp[pl.ds((local + e) * L, L), :] = low
    state = []
    for t in range(L // 8):
        block = jnp.where(lane_index < L, grams[0][t * 8 : t * 8 + 8], grams[1][t * 8 : t * 8 + 8])
        state.append(jnp.where(lane_index % L == sub_index + t * 8, block + 1.0, block))
    owed = peer_positions(lax.axis_index("energy"), position, jnp.where, out.shape[0])
    pick = jnp.concatenate(
        [(lane_index == sub_index + lax.rem(at, BS // 8) * 8).astype(f32) for at in owed], 0
    )
    near_block = pl.multiple_of(lax.div(position, BS // 8) * BS, BS)
    mine = dot_nt(pick.astype(bf16), big[pl.ds(2 * BS, 2 * BS), pl.ds(near_block, BS)])
    mine = mine[:, :BS] + mine[:, BS:]
    half = (lane_index // L) * L

    unit = (lane_index % 8 == sub_index).astype(f32)
    lowers, inverses_of = [], []
    inside = [spread_lane(state[0], half + n) for n in range(8)]
    for block in range(L // 8):
        column = half + block * 8
        factors = [
            [spread_lane(state[t], column + n) for n in range(8)] for t in range(block + 1, len(state))
        ]
        beside = list(factors[0]) if block < 7 else [jnp.zeros_like(unit)] * 8
        following = [spread_lane(state[block + 1], column + 8 + n) for n in range(8)] if block < 7 else []
        within = lane_index % L // 8 == block
        before = lane_index % L < block * 8
        rows = jnp.where(within, unit, state[block])
        lowers.append(jnp.where(before | within, rows, 0.0))
        for n in range(0, 8, 2):
            first, cross, second = (
                spread_row(inside[n], n), spread_row(inside[n], n + 1), spread_row(inside[n + 1], n + 1)
            )
            inverse = 1.0 / (first * second - cross * cross)
            first, cross, second = first * inverse, cross * inverse, second * inverse

            def solve(x, y):
                return second * x - cross * y, first * y - cross * x

            for m in range(n + 2, 8):
                x, y = solve(spread_row(inside[m], n), spread_row(inside[m], n + 1))
                left = inside[m] - (inside[n] * x + inside[n + 1] * y)
                inside[m] = jnp.where(sub_index == n, x, jnp.where(sub_index == n + 1, y, left))
                beside[m] = beside[m] - (beside[n] * x + beside[n + 1] * y)
            upper, lower = solve(beside[n], beside[n + 1])
            for m in range(len(following)):
                following[m] = following[m] - (
                    upper * spread_row(beside[n], m) + lower * spread_row(beside[n + 1], m)
                )
            x, y = solve(spread_row(rows, n), spread_row(rows, n + 1))
            left = rows - (inside[n] * x + inside[n + 1] * y)
            rows = jnp.where(sub_index == n, x, jnp.where(sub_index == n + 1, y, left))
        inside = following
        inverses_of.append(jnp.where(before | within, rows, 0.0))
        solved = [spread_row(rows, n) for n in range(8)]
        for t in range(block + 1, len(state)):
            kept = jnp.where(within, 0.0, state[t])
            for n in range(8):
                kept = kept - factors[t - block - 1][n] * solved[n]
            state[t] = kept

    owner = lax.axis_index("energy")
    chosen = [jnp.int32(-1) for _ in range(slots.shape[0])]
    count = jnp.int32(0)
    for index in range(owners.shape[1]):
        hit = owners[0, index] == owner
        for c in range(len(chosen)):
            chosen[c] = jnp.where(hit & (count == c), index, chosen[c])
        count = count + hit.astype(jnp.int32)
    for c in range(len(chosen)):
        slots[c] = jnp.full(slots.shape[1:], chosen[c], jnp.int32)

    sides = []
    for n, part in enumerate(split(jnp.concatenate(lowers, 0))):
        for copy in range(2):
            turned[pl.ds(copy * L, L), pl.ds(n * BS, BS)] = part
    high, low = split(mine)
    lanes = lax.broadcasted_iota(jnp.int32, (L, BS), 1)
    none = jnp.zeros_like(high)
    for e in range(local):
        own = lanes // L == e
        left = jnp.concatenate(
            [
                jnp.concatenate([jnp.where(own, high, none)] * 2, 1),
                jnp.concatenate([jnp.where(own, low, none), none], 1),
            ],
            0,
        )
        across = dot_nt(left, turned[...])
        sides.append(across[:L] + across[L:])
    for g in range(2):
        tall = jnp.concatenate(inverses_of[g * 4 : g * 4 + 4], 0)
        tall_lanes = lax.broadcasted_iota(jnp.int32, tall.shape, 1)
        parts = []
        for e in range(local):
            high, low = split(jnp.where(tall_lanes // L == e, tall, 0.0))
            parts.append(jnp.concatenate([high, high], 1))
            parts.append(jnp.concatenate([low, jnp.zeros_like(low)], 1))
        full = dot_nn(jnp.concatenate(parts, 0), bp[...])
        for e in range(local):
            high, low = split(full[e * L : e * L + 32] + full[e * L + 32 : e * L + 64])
            ahead_rows[e, pl.ds(g * 32, 32), :] = high
            ahead_rows[e, pl.ds(L + g * 32, 32), :] = low
    for e in range(local):
        high, low = split(sides[e])
        left = jnp.concatenate([high, jnp.where(lanes < L, low, none)], 0)
        full = dot_nn(left, ahead_rows[e])
        sigma = (full[:L] + full[L:]) * (1.0 / L)
        for peer in range(out.shape[0]):
            out[peer, e] = sigma[peer * 8 : peer * 8 + 8].astype(bf16)

def place_kernel(incoming, slots, out):
    groups, local, rows, columns = incoming.shape
    zeros = jnp.zeros((rows, columns), out.dtype)
    sources = [incoming[n // local, n % local].astype(f32) for n in range(groups * local)]
    for c in range(out.shape[1]):
        index = jnp.concatenate([slots[c]] * (columns // BS), 1)
        total = jnp.zeros((rows, columns), f32)
        for n, source in enumerate(sources):
            total = jnp.where(index == n, source, total)
        out[0, c, 0] = total.astype(out.dtype)
        out[0, c, 1] = zeros


def body(energies, onsite, blocks, pattern, probes, ranks, owner_map):
    local = energies.shape[0]
    groups = lax.axis_size("energy")
    rows = NC // lax.axis_size("contour")
    row_blocks = blocks.shape[0]
    vmem = pl.BlockSpec(memory_space=pltpu.VMEM)
    anywhere = pl.BlockSpec(memory_space=pl.ANY)
    arrays = (
        energies, ranks, onsite.reshape(row_blocks, BS), pattern.T, owner_map.T, probes, blocks
    )
    sigma, slots = pl.pallas_call(
        sigma_kernel,
        out_shape=(
            pltpu.VMEM((groups, local, rows, NC), bf16),
            pltpu.VMEM((local + 1, rows, BS), jnp.int32),
        ),
        in_specs=[anywhere] * len(arrays),
        out_specs=(vmem, vmem),
        scratch_shapes=[
            pltpu.SMEM(energies.shape, f32),
            pltpu.SMEM(ranks.shape, jnp.int32),
            pltpu.VMEM((row_blocks, BS), f32),
            pltpu.SMEM((KB, row_blocks), jnp.int32),
            pltpu.SMEM((1, owner_map.shape[0]), jnp.int32),
            pltpu.VMEM(probes.shape, bf16),
            pltpu.VMEM((NEAR, BS, KB * BS), bf16),
            pltpu.VMEM((NEAR, 2 * local * BS, KB * BS), bf16),
            pltpu.VMEM((NEAR, (1 + local) * L, KB * BS), bf16),
            pltpu.VMEM((4 * local * L, NC), bf16),
            pltpu.VMEM((2 * local * L, NC), bf16),
            pltpu.VMEM((NEAR * BS, BS), bf16),
            pltpu.VMEM((NEAR, BS, KB * BS), bf16),
            pltpu.VMEM((NEAR, 4 * BS, KB * BS), f32),
            pltpu.VMEM((2 * L, 2 * BS), bf16),
            pltpu.VMEM((local, 2 * L, NC), bf16),
            pltpu.SemaphoreType.DMA((6 + NEAR,)),
        ],
        compiler_params=pltpu.CompilerParams(vmem_limit_bytes=32 * 2**20),
        name="sigma",
    )(*(pltpu.with_memory_space_constraint(array, pltpu.HBM) for array in arrays))
    exchange = exchange_groups(groups, lax.axis_size("contour"))
    incoming = lax.all_to_all(sigma, ("energy", "contour"), 0, 0, axis_index_groups=exchange)
    return pl.pallas_call(
        place_kernel,
        out_shape=jax.ShapeDtypeStruct((1, local + 1, 2, rows, NC), bf16),
        in_specs=[vmem, vmem],
        out_specs=vmem,
        name="place",
    )(
        pltpu.with_memory_space_constraint(incoming, pltpu.VMEM),
        pltpu.with_memory_space_constraint(slots, pltpu.VMEM),
    )


def solution(mesh):
    placed = (P("energy"), P(), P(), P(), P(), P("energy"), P())
    return jax.shard_map(
        body,
        mesh=mesh,
        in_specs=placed,
        out_specs=P("energy", None, None, "contour", None),
        check_vma=False,
    )
```

```python
import jax
import jax.numpy as jnp
from jax import lax
from jax.experimental import pallas as pl
from jax.experimental.pallas import tpu as pltpu
from jax.sharding import PartitionSpec as P


L = 64
NC = 512
BS = 128
KB = 3
CHAIN = (0, 2, 6)
NEAR = NC // BS
f32 = jnp.float32
bf16 = jnp.bfloat16

def follow(home, step, choose):
    out = home
    for n, at in enumerate(CHAIN):
        out = choose(home == at, CHAIN[(n + step) % len(CHAIN)], out)
    return out


def other_core(group, home):
    return group % 4 // 2 * ((home > 0))


def peer_positions(group, position, choose, groups):
    core = position % 2
    home = choose((group == 0) & (core == 0), follow(position - core, -1, choose), position - core)
    parity = (core + other_core(group, home)) % 2
    out = []
    for peer in range(groups):
        place = choose(parity == 0, follow(home, 1, choose), home) if peer == 0 else home
        out.append(place + (parity + other_core(peer, home)) % 2)
    return out


def exchange_groups(groups, positions):
    found = []
    for position in range(positions):
        at = peer_positions(0, position, lambda test, yes, no: yes if test else no, groups)
        found.append([group * positions + at[group] for group in range(groups)])
    return found


def dot_nt(left, right):
    return lax.dot_general(left, right, (((1,), (1,)), ((), ())), preferred_element_type=f32)

def dot_nn(left, right):
    return lax.dot_general(left, right, (((1,), (0,)), ((), ())), preferred_element_type=f32)

def dot_tn(left, right):
    return lax.dot_general(left, right, (((0,), (0,)), ((), ())), preferred_element_type=f32)


def split(x):
    high = x.astype(bf16)
    return high, (x - high.astype(f32)).astype(bf16)

def spread_lane(x, lanes):
    return jnp.take_along_axis(x, lanes, axis=1)


def spread_row(x, row, rows=8):
    return jnp.broadcast_to(x[row : row + 1, :], (rows, x.shape[1]))


def split_wide(x):
    high = x.astype(bf16).astype(f32)
    return high, x - high


def ladder(x, exponent):
    square = x * x
    fourth = square * square
    out = jnp.where(exponent % 2 == 1, x, 1.0)
    out = jnp.where(exponent // 2 % 2 == 1, out * square, out)
    out = jnp.where(exponent // 4 == 1, out * fourth, out)
    return out, fourth * fourth


def powers(base):
    out = [base]
    for _ in range(6):
        out.append(out[-1] * out[-1])
    return out

def sigma_kernel(
    energies_in, ranks_in, onsite_in, pattern_in, owners_in, probes, blocks, out, slots,
    energies, ranks, onsite, pattern, owners, pr, bl, mix, near_terms, big, bp,
    left_rows, right_rows, products, turned, ahead_rows, sems,
):
    local = energies.shape[0]
    small_copies = [
        pltpu.make_async_copy(source, target, sems.at[n])
        for n, (source, target) in enumerate(
            (
                (onsite_in, onsite),
                (pattern_in, pattern),
                (energies_in, energies),
                (ranks_in, ranks),
                (owners_in, owners),
            )
        )
    ]
    block_copies = [
        pltpu.make_async_copy(
            blocks.at[pl.ds(0, NEAR), k], bl.at[:, :, pl.ds(k * BS, BS)], sems.at[6 + k]
        )
        for k in range(KB)
    ]
    probe_copy = pltpu.make_async_copy(probes, pr, sems.at[5])
    for copy in small_copies + block_copies + [probe_copy]:
        copy.start()
    position = lax.axis_index("contour")
    sub_index = lax.broadcasted_iota(jnp.int32, (8, BS), 0)
    lane_index = lax.broadcasted_iota(jnp.int32, (8, BS), 1)

    for copy in small_copies:
        copy.wait()
    all_weights = []
    for i in range(NEAR):
        near = spread_row(onsite[pl.ds(i, 1), :], 0, 8)
        for e in range(local):
            low_order, raised = ladder(near - energies[e], sub_index)
            high_order, _ = ladder(raised, sub_index)
            for h, table in enumerate((low_order, high_order)):
                high, low = split_wide(table)
                at = i * BS + (e * 2 + h) * 32
                left_rows[pl.ds(at, 32), :] = jnp.concatenate([high, high, low, low], 0).astype(bf16)
    def power_block(i):
        weights = []
        for k in range(KB):
            far = spread_row(onsite[pl.ds(pattern[k, i], 1), :], 0, 8)
            for e in range(local):
                low_order, raised = ladder(far - energies[e], 7 - sub_index)
                high_order, last = ladder(raised, 7 - sub_index)
                weight = 1.0 / (1.0 + last)
                weights.append(weight)
                for h, table in enumerate((low_order, high_order * weight)):
                    high, low = split_wide(table)
                    right_rows[i, pl.ds((e * 2 + h) * 32, 32), pl.ds(k * BS, BS)] = jnp.concatenate(
                        [high, low, high, low], 0
                    ).astype(bf16)
        for g in range(2 * local):
            products[i, pl.ds(g * BS, BS), :] = dot_tn(
                left_rows[pl.ds(i * BS + g * 32, 32), :], right_rows[i, pl.ds(g * 32, 32), :]
            )
        all_weights.append(weights)
    for i in range(NEAR):
        power_block(i)
    for copy in block_copies:
        copy.wait()
    def mix_block(i):
        for k in range(KB):
            for r in range(BS // 16):
                coupling = bl[i, pl.ds(r * 16, 16), pl.ds(k * BS, BS)].astype(f32)
                for e in range(local):
                    low_order = products[i, pl.ds(e * 2 * BS + r * 16, 16), pl.ds(k * BS, BS)]
                    high_order = products[i, pl.ds((e * 2 + 1) * BS + r * 16, 16), pl.ds(k * BS, BS)]
                    high, low = split(coupling * (low_order * high_order))
                    for n, part in enumerate((high, low)):
                        mix[i, pl.ds(e * BS + r * 16, 16), pl.ds((n * KB + k) * BS, BS)] = part

    def gather_terms(i):
        for k in range(KB):
            far = pr[:, pl.ds(pl.multiple_of(pattern[k, i] * BS, BS), BS)]
            for n in range(2):
                near_terms[i, pl.ds(0, L), pl.ds((n * KB + k) * BS, BS)] = far
            far = far.astype(f32).reshape(8, 8, BS)
            for e in range(local):
                scaled = far * all_weights[i][k * local + e][None]
                near_terms[i, pl.ds((1 + e) * L, L), pl.ds(k * BS, BS)] = scaled.reshape(L, BS).astype(bf16)

    def couple(i):
        return (
            dot_nt(near_terms[i, pl.ds(0, L), :], mix[i]),
            dot_nt(near_terms[i, pl.ds(L, local * L), pl.ds(0, KB * BS)], bl[i]),
        )

    def finish(i, coupled, plain):
        near = jnp.broadcast_to(onsite[pl.ds(i, 1), :], (8, BS))
        source = pr[:, pl.ds(i * BS, BS)].astype(f32).reshape(8, 8, BS)
        for e in range(local):
            mixed = coupled[:, e * BS : (e + 1) * BS].reshape(8, 8, BS)
            shift = near - energies[e]
            weight = 1.0 / (1.0 + powers(shift)[6])
            first = weight[None] * (source - mixed)
            second = shift[None] * first + plain[e * L : (e + 1) * L].reshape(8, 8, BS)
            kept = (
                lax.broadcasted_iota(jnp.int32, (8, 8, BS), 0) * 8
                + lax.broadcasted_iota(jnp.int32, (8, 8, BS), 1)
            ) < ranks[e]
            first = jnp.where(kept, first, 0.0).reshape(L, BS)
            second = jnp.where(kept, second, 0.0).reshape(L, BS)
            for n, part in enumerate(split(first) + split(second)):
                big[pl.ds((n * local + e) * L, L), pl.ds(i * BS, BS)] = part

    probe_copy.wait()
    pending = None
    for i in range(NEAR):
        mix_block(i)
        gather_terms(i)
        done = couple(i)
        if pending is not None:
            finish(i - 1, *pending)
        pending = done
    finish(NEAR - 1, *pending)

    near_high, near_low = big[pl.ds(0, BS), :], big[pl.ds(BS, BS), :]
    wide = dot_nt(near_high, big[pl.ds(0, 2 * BS), :])
    square = (wide[:, :BS] + (wide[:, BS:] + dot_nt(near_low, near_high))) * (1.0 / NC)
    far = dot_nt(big[pl.ds(0, 2 * BS), :], big[pl.ds(2 * BS, BS), :])
    across = (far[:BS] + (far[BS:] + dot_nt(near_high, big[pl.ds(3 * BS, BS), :]))) * (1.0 / NC)
    grams = []
    for e in range(local):
        grams.append(square[e * L : (e + 1) * L])
        cross = across[e * L : (e + 1) * L]
        lanes = lax.broadcasted_iota(jnp.int32, (L, BS), 1)
        high, low = split(jnp.where(lanes // L == e, cross, 0.0))
        left = jnp.concatenate(
            [jnp.concatenate([high, high], 1), jnp.concatenate([low, jnp.zeros_like(low)], 1)], 0
        )
        applied = dot_nn(left, big[pl.ds(0, 2 * BS), :])
        high, low = split(applied[:L] + applied[L:])
        bp[pl.ds(e * L, L), :] = high
        bp[pl.ds((local + e) * L, L), :] = low
    state = []
    for t in range(L // 8):
        block = jnp.where(lane_index < L, grams[0][t * 8 : t * 8 + 8], grams[1][t * 8 : t * 8 + 8])
        state.append(jnp.where(lane_index % L == sub_index + t * 8, block + 1.0, block))
    owed = peer_positions(lax.axis_index("energy"), position, jnp.where, out.shape[0])
    owed = [owed[0], owed[1], owed[2], owed[2]]
    pick = jnp.concatenate(
        [(lane_index == sub_index + lax.rem(at, BS // 8) * 8).astype(f32) for at in owed], 0
    )
    near_block = pl.multiple_of(lax.div(position, BS // 8) * BS, BS)
    mine = dot_nt(pick.astype(bf16), big[pl.ds(2 * BS, 2 * BS), pl.ds(near_block, BS)])
    mine = mine[:, :BS] + mine[:, BS:]
    half = (lane_index // L) * L

    height = 8 * len(owed)
    lanes = lax.broadcasted_iota(jnp.int32, (height, BS), 1)
    none = jnp.zeros((height, BS), bf16)

    def apply_left():
        for n, part in enumerate(split(jnp.concatenate(lowers, 0))):
            for copy in range(2):
                turned[pl.ds(copy * L, L), pl.ds(n * BS, BS)] = part
        high, low = split(mine)
        out = []
        for e in range(local):
            own = lanes // L == e
            left = jnp.concatenate(
                [
                    jnp.concatenate([jnp.where(own, high, none)] * 2, 1),
                    jnp.concatenate([jnp.where(own, low, none), none], 1),
                ],
                0,
            )
            across = dot_nt(left, turned[...])
            out.append(across[:height] + across[height:])
        return out

    def apply_right(first, count):
        tall = jnp.concatenate(inverses_of[first : first + count], 0)
        size = count * 8
        tall_lanes = lax.broadcasted_iota(jnp.int32, tall.shape, 1)
        parts = []
        for e in range(local):
            high, low = split(jnp.where(tall_lanes // L == e, tall, 0.0))
            parts.append(jnp.concatenate([high, high], 1))
            parts.append(jnp.concatenate([low, jnp.zeros_like(low)], 1))
        full = dot_nn(jnp.concatenate(parts, 0), bp[...])
        for e in range(local):
            at = 2 * e * size
            high, low = split(full[at : at + size] + full[at + size : at + 2 * size])
            ahead_rows[e, pl.ds(first * 8, size), :] = high
            ahead_rows[e, pl.ds(L + first * 8, size), :] = low

    owner = lax.axis_index("energy")
    chosen = [jnp.int32(-1) for _ in range(slots.shape[0])]
    count = jnp.int32(0)
    for index in range(owners.shape[1]):
        hit = owners[0, index] == owner
        for c in range(len(chosen)):
            chosen[c] = jnp.where(hit & (count == c), index, chosen[c])
        count = count + hit.astype(jnp.int32)
    for c in range(len(chosen)):
        slots[c] = jnp.full(slots.shape[1:], chosen[c], jnp.int32)

    sides = []
    lowers, inverses_of = [], []
    unit = (lane_index % 8 == sub_index).astype(f32)
    inside = [spread_lane(state[0], half + n) for n in range(8)]
    for block in range(L // 8):
        column = half + block * 8
        factors = [
            [spread_lane(state[t], column + n) for n in range(8)] for t in range(block + 1, len(state))
        ]
        beside = list(factors[0]) if block < 7 else [jnp.zeros_like(unit)] * 8
        following = [spread_lane(state[block + 1], column + 8 + n) for n in range(8)] if block < 7 else []
        within = lane_index % L // 8 == block
        before = lane_index % L < block * 8
        rows = jnp.where(within, unit, state[block])
        lowers.append(jnp.where(before | within, rows, 0.0))
        if block == L // 8 - 1:
            sides = apply_left()
        for n in range(0, 8, 2):
            first, cross, second = (
                spread_row(inside[n], n), spread_row(inside[n], n + 1), spread_row(inside[n + 1], n + 1)
            )
            inverse = 1.0 / (first * second - cross * cross)
            first, cross, second = first * inverse, cross * inverse, second * inverse

            def solve(x, y):
                return second * x - cross * y, first * y - cross * x

            for m in range(n + 2, 8):
                x, y = solve(spread_row(inside[m], n), spread_row(inside[m], n + 1))
                left = inside[m] - (inside[n] * x + inside[n + 1] * y)
                inside[m] = jnp.where(sub_index == n, x, jnp.where(sub_index == n + 1, y, left))
                beside[m] = beside[m] - (beside[n] * x + beside[n + 1] * y)
            upper, lower = solve(beside[n], beside[n + 1])
            for m in range(len(following)):
                following[m] = following[m] - (
                    upper * spread_row(beside[n], m) + lower * spread_row(beside[n + 1], m)
                )
            x, y = solve(spread_row(rows, n), spread_row(rows, n + 1))
            left = rows - (inside[n] * x + inside[n + 1] * y)
            rows = jnp.where(sub_index == n, x, jnp.where(sub_index == n + 1, y, left))
        inside = following
        inverses_of.append(jnp.where(before | within, rows, 0.0))
        if block >= 1 and (block - 1) % 2 == 0:
            apply_right(block - 1, 2)
        solved = [spread_row(rows, n) for n in range(8)]
        for t in range(block + 1, len(state)):
            kept = jnp.where(within, 0.0, state[t])
            for n in range(8):
                kept = kept - factors[t - block - 1][n] * solved[n]
            state[t] = kept

    for first in ():
        apply_right(first, 2)
    for e in range(local):
        high, low = split(sides[e])
        left = jnp.concatenate([high, jnp.where(lanes < L, low, none)], 0)
        full = dot_nn(left, ahead_rows[e])
        sigma = (full[:height] + full[height:]) * (1.0 / L)
        rows = [sigma[n * 8 : n * 8 + 8].astype(bf16) for n in range(3)]
        for peer in range(out.shape[0]):
            out[peer, e] = rows[0 if peer == 0 else 1 + peer % 4 // 2]

def place_kernel(incoming, slots, out):
    groups, local, rows, columns = incoming.shape
    zeros = jnp.zeros((rows, columns), out.dtype)
    sources = [incoming[n // local, n % local].astype(f32) for n in range(groups * local)]
    for c in range(out.shape[1]):
        index = jnp.concatenate([slots[c]] * (columns // BS), 1)
        total = jnp.zeros((rows, columns), f32)
        for n, source in enumerate(sources):
            total = jnp.where(index == n, source, total)
        out[0, c, 0] = total.astype(out.dtype)
        out[0, c, 1] = zeros


def body(energies, onsite, blocks, pattern, probes, ranks, owner_map):
    local = energies.shape[0]
    groups = lax.axis_size("energy")
    rows = NC // lax.axis_size("contour")
    row_blocks = blocks.shape[0]
    vmem = pl.BlockSpec(memory_space=pltpu.VMEM)
    anywhere = pl.BlockSpec(memory_space=pl.ANY)
    arrays = (
        energies, ranks, onsite.reshape(row_blocks, BS), pattern.T, owner_map.T, probes, blocks
    )
    sigma, slots = pl.pallas_call(
        sigma_kernel,
        out_shape=(
            pltpu.VMEM((groups, local, rows, NC), bf16),
            pltpu.VMEM((local + 1, rows, BS), jnp.int32),
        ),
        in_specs=[anywhere] * len(arrays),
        out_specs=(vmem, vmem),
        scratch_shapes=[
            pltpu.SMEM(energies.shape, f32),
            pltpu.SMEM(ranks.shape, jnp.int32),
            pltpu.VMEM((row_blocks, BS), f32),
            pltpu.SMEM((KB, row_blocks), jnp.int32),
            pltpu.SMEM((1, owner_map.shape[0]), jnp.int32),
            pltpu.VMEM(probes.shape, bf16),
            pltpu.VMEM((NEAR, BS, KB * BS), bf16),
            pltpu.VMEM((NEAR, local * BS, 2 * KB * BS), bf16),
            pltpu.VMEM((NEAR, (1 + local) * L, 2 * KB * BS), bf16),
            pltpu.VMEM((4 * local * L, NC), bf16),
            pltpu.VMEM((2 * local * L, NC), bf16),
            pltpu.VMEM((NEAR * BS, BS), bf16),
            pltpu.VMEM((NEAR, BS, KB * BS), bf16),
            pltpu.VMEM((NEAR, 4 * BS, KB * BS), f32),
            pltpu.VMEM((2 * L, 2 * BS), bf16),
            pltpu.VMEM((local, 2 * L, NC), bf16),
            pltpu.SemaphoreType.DMA((6 + NEAR,)),
        ],
        compiler_params=pltpu.CompilerParams(vmem_limit_bytes=32 * 2**20),
        name="sigma",
    )(*(pltpu.with_memory_space_constraint(array, pltpu.HBM) for array in arrays))
    exchange = exchange_groups(groups, lax.axis_size("contour"))
    incoming = lax.all_to_all(sigma, ("energy", "contour"), 0, 0, axis_index_groups=exchange)
    return pl.pallas_call(
        place_kernel,
        out_shape=jax.ShapeDtypeStruct((1, local + 1, 2, rows, NC), bf16),
        in_specs=[vmem, vmem],
        out_specs=vmem,
        name="place",
    )(
        pltpu.with_memory_space_constraint(incoming, pltpu.VMEM),
        pltpu.with_memory_space_constraint(slots, pltpu.VMEM),
    )


def solution(mesh):
    placed = (P("energy"), P(), P(), P(), P(), P("energy"), P())
    return jax.shard_map(
        body,
        mesh=mesh,
        in_specs=placed,
        out_specs=P("energy", None, None, "contour", None),
        check_vma=False,
    )
```

```python
import jax
import jax.numpy as jnp
from jax import lax
from jax.experimental import pallas as pl
from jax.experimental.pallas import tpu as pltpu
from jax.sharding import PartitionSpec as P


L = 64
NC = 512
BS = 128
KB = 3
CHAIN = (0, 4, 8)
NEAR = NC // BS
f32 = jnp.float32
bf16 = jnp.bfloat16

def follow(home, step, choose):
    out = home
    for n, at in enumerate(CHAIN):
        out = choose(home == at, CHAIN[(n + step) % len(CHAIN)], out)
    return out


def other_core(group, home):
    return group % 4 // 2 * ((home > 0))


def peer_positions(group, position, choose, groups):
    core = position % 2
    home = choose((group == 0) & (core == 0), follow(position - core, -1, choose), position - core)
    parity = (core + other_core(group, home)) % 2
    out = []
    for peer in range(groups):
        place = choose(parity == 0, follow(home, 1, choose), home) if peer == 0 else home
        out.append(place + (parity + other_core(peer, home)) % 2)
    return out


def exchange_groups(groups, positions):
    found = []
    for position in range(positions):
        at = peer_positions(0, position, lambda test, yes, no: yes if test else no, groups)
        found.append([group * positions + at[group] for group in range(groups)])
    return found


def dot_nt(left, right):
    return lax.dot_general(left, right, (((1,), (1,)), ((), ())), preferred_element_type=f32)

def dot_nn(left, right):
    return lax.dot_general(left, right, (((1,), (0,)), ((), ())), preferred_element_type=f32)

def dot_tn(left, right):
    return lax.dot_general(left, right, (((0,), (0,)), ((), ())), preferred_element_type=f32)


def split(x):
    high = x.astype(bf16)
    return high, (x - high.astype(f32)).astype(bf16)

def spread_lane(x, lanes):
    return jnp.take_along_axis(x, lanes, axis=1)


def spread_row(x, row, rows=8):
    return jnp.broadcast_to(x[row : row + 1, :], (rows, x.shape[1]))


def split_wide(x):
    high = x.astype(bf16).astype(f32)
    return high, x - high


def ladder(x, exponent):
    square = x * x
    fourth = square * square
    out = jnp.where(exponent % 2 == 1, x, 1.0)
    out = jnp.where(exponent // 2 % 2 == 1, out * square, out)
    out = jnp.where(exponent // 4 == 1, out * fourth, out)
    return out, fourth * fourth


def powers(base):
    out = [base]
    for _ in range(6):
        out.append(out[-1] * out[-1])
    return out

def sigma_kernel(
    energies_in, ranks_in, onsite_in, pattern_in, owners_in, probes, blocks, out, slots,
    energies, ranks, onsite, pattern, owners, pr, bl, mix, near_terms, big, bp,
    left_rows, right_rows, products, turned, ahead_rows, sems,
):
    local = energies.shape[0]
    small_copies = [
        pltpu.make_async_copy(source, target, sems.at[n])
        for n, (source, target) in enumerate(
            (
                (onsite_in, onsite),
                (pattern_in, pattern),
                (energies_in, energies),
                (ranks_in, ranks),
                (owners_in, owners),
            )
        )
    ]
    block_copies = [
        pltpu.make_async_copy(
            blocks.at[pl.ds(0, NEAR), k], bl.at[:, :, pl.ds(k * BS, BS)], sems.at[6 + k]
        )
        for k in range(KB)
    ]
    probe_copy = pltpu.make_async_copy(probes, pr, sems.at[5])
    for copy in small_copies + block_copies + [probe_copy]:
        copy.start()
    position = lax.axis_index("contour")
    sub_index = lax.broadcasted_iota(jnp.int32, (8, BS), 0)
    lane_index = lax.broadcasted_iota(jnp.int32, (8, BS), 1)

    for copy in small_copies:
        copy.wait()
    all_weights = []
    for i in range(NEAR):
        near = spread_row(onsite[pl.ds(i, 1), :], 0, 8)
        for e in range(local):
            low_order, raised = ladder(near - energies[e], sub_index)
            high_order, _ = ladder(raised, sub_index)
            for h, table in enumerate((low_order, high_order)):
                high, low = split_wide(table)
                at = i * BS + (e * 2 + h) * 32
                left_rows[pl.ds(at, 32), :] = jnp.concatenate([high, high, low, low], 0).astype(bf16)
    def power_block(i):
        weights = []
        for k in range(KB):
            far = spread_row(onsite[pl.ds(pattern[k, i], 1), :], 0, 8)
            for e in range(local):
                low_order, raised = ladder(far - energies[e], 7 - sub_index)
                high_order, last = ladder(raised, 7 - sub_index)
                weight = 1.0 / (1.0 + last)
                weights.append(weight)
                for h, table in enumerate((low_order, high_order * weight)):
                    high, low = split_wide(table)
                    right_rows[i, pl.ds((e * 2 + h) * 32, 32), pl.ds(k * BS, BS)] = jnp.concatenate(
                        [high, low, high, low], 0
                    ).astype(bf16)
        for g in range(2 * local):
            products[i, pl.ds(g * BS, BS), :] = dot_tn(
                left_rows[pl.ds(i * BS + g * 32, 32), :], right_rows[i, pl.ds(g * 32, 32), :]
            )
        all_weights.append(weights)
    for i in range(NEAR):
        power_block(i)
    for copy in block_copies:
        copy.wait()
    def mix_block(i):
        for k in range(KB):
            for r in range(BS // 16):
                coupling = bl[i, pl.ds(r * 16, 16), pl.ds(k * BS, BS)].astype(f32)
                for e in range(local):
                    low_order = products[i, pl.ds(e * 2 * BS + r * 16, 16), pl.ds(k * BS, BS)]
                    high_order = products[i, pl.ds((e * 2 + 1) * BS + r * 16, 16), pl.ds(k * BS, BS)]
                    high, low = split(coupling * (low_order * high_order))
                    for n, part in enumerate((high, low)):
                        mix[i, pl.ds(e * BS + r * 16, 16), pl.ds((n * KB + k) * BS, BS)] = part

    def gather_terms(i):
        for k in range(KB):
            far = pr[:, pl.ds(pl.multiple_of(pattern[k, i] * BS, BS), BS)]
            for n in range(2):
                near_terms[i, pl.ds(0, L), pl.ds((n * KB + k) * BS, BS)] = far
            far = far.astype(f32).reshape(8, 8, BS)
            for e in range(local):
                scaled = far * all_weights[i][k * local + e][None]
                near_terms[i, pl.ds((1 + e) * L, L), pl.ds(k * BS, BS)] = scaled.reshape(L, BS).astype(bf16)

    def couple(i):
        return (
            dot_nt(near_terms[i, pl.ds(0, L), :], mix[i]),
            dot_nt(near_terms[i, pl.ds(L, local * L), pl.ds(0, KB * BS)], bl[i]),
        )

    def finish(i, coupled, plain):
        near = jnp.broadcast_to(onsite[pl.ds(i, 1), :], (8, BS))
        source = pr[:, pl.ds(i * BS, BS)].astype(f32).reshape(8, 8, BS)
        for e in range(local):
            mixed = coupled[:, e * BS : (e + 1) * BS].reshape(8, 8, BS)
            shift = near - energies[e]
            weight = 1.0 / (1.0 + powers(shift)[6])
            first = weight[None] * (source - mixed)
            second = shift[None] * first + plain[e * L : (e + 1) * L].reshape(8, 8, BS)
            kept = (
                lax.broadcasted_iota(jnp.int32, (8, 8, BS), 0) * 8
                + lax.broadcasted_iota(jnp.int32, (8, 8, BS), 1)
            ) < ranks[e]
            first = jnp.where(kept, first, 0.0).reshape(L, BS)
            second = jnp.where(kept, second, 0.0).reshape(L, BS)
            for n, part in enumerate(split(first) + split(second)):
                big[pl.ds((n * local + e) * L, L), pl.ds(i * BS, BS)] = part

    probe_copy.wait()
    pending = None
    for i in range(NEAR):
        mix_block(i)
        gather_terms(i)
        done = couple(i)
        if pending is not None:
            finish(i - 1, *pending)
        pending = done
    finish(NEAR - 1, *pending)

    near_high, near_low = big[pl.ds(0, BS), :], big[pl.ds(BS, BS), :]
    wide = dot_nt(near_high, big[pl.ds(0, 2 * BS), :])
    square = (wide[:, :BS] + (wide[:, BS:] + dot_nt(near_low, near_high))) * (1.0 / NC)
    far = dot_nt(big[pl.ds(0, 2 * BS), :], big[pl.ds(2 * BS, BS), :])
    across = (far[:BS] + (far[BS:] + dot_nt(near_high, big[pl.ds(3 * BS, BS), :]))) * (1.0 / NC)
    grams = []
    for e in range(local):
        grams.append(square[e * L : (e + 1) * L])
        cross = across[e * L : (e + 1) * L]
        lanes = lax.broadcasted_iota(jnp.int32, (L, BS), 1)
        high, low = split(jnp.where(lanes // L == e, cross, 0.0))
        left = jnp.concatenate(
            [jnp.concatenate([high, high], 1), jnp.concatenate([low, jnp.zeros_like(low)], 1)], 0
        )
        applied = dot_nn(left, big[pl.ds(0, 2 * BS), :])
        high, low = split(applied[:L] + applied[L:])
        bp[pl.ds(e * L, L), :] = high
        bp[pl.ds((local + e) * L, L), :] = low
    state = []
    for t in range(L // 8):
        block = jnp.where(lane_index < L, grams[0][t * 8 : t * 8 + 8], grams[1][t * 8 : t * 8 + 8])
        state.append(jnp.where(lane_index % L == sub_index + t * 8, block + 1.0, block))
    owed = peer_positions(lax.axis_index("energy"), position, jnp.where, out.shape[0])
    owed = [owed[0], owed[1], owed[2], owed[2]]
    pick = jnp.concatenate(
        [(lane_index == sub_index + lax.rem(at, BS // 8) * 8).astype(f32) for at in owed], 0
    )
    near_block = pl.multiple_of(lax.div(position, BS // 8) * BS, BS)
    mine = dot_nt(pick.astype(bf16), big[pl.ds(2 * BS, 2 * BS), pl.ds(near_block, BS)])
    mine = mine[:, :BS] + mine[:, BS:]
    half = (lane_index // L) * L

    height = 8 * len(owed)
    lanes = lax.broadcasted_iota(jnp.int32, (height, BS), 1)
    none = jnp.zeros((height, BS), bf16)

    def apply_left():
        for n, part in enumerate(split(jnp.concatenate(lowers, 0))):
            for copy in range(2):
                turned[pl.ds(copy * L, L), pl.ds(n * BS, BS)] = part
        high, low = split(mine)
        out = []
        for e in range(local):
            own = lanes // L == e
            left = jnp.concatenate(
                [
                    jnp.concatenate([jnp.where(own, high, none)] * 2, 1),
                    jnp.concatenate([jnp.where(own, low, none), none], 1),
                ],
                0,
            )
            across = dot_nt(left, turned[...])
            out.append(across[:height] + across[height:])
        return out

    def apply_right(first, count):
        tall = jnp.concatenate(inverses_of[first : first + count], 0)
        size = count * 8
        tall_lanes = lax.broadcasted_iota(jnp.int32, tall.shape, 1)
        parts = []
        for e in range(local):
            high, low = split(jnp.where(tall_lanes // L == e, tall, 0.0))
            parts.append(jnp.concatenate([high, high], 1))
            parts.append(jnp.concatenate([low, jnp.zeros_like(low)], 1))
        full = dot_nn(jnp.concatenate(parts, 0), bp[...])
        for e in range(local):
            at = 2 * e * size
            high, low = split(full[at : at + size] + full[at + size : at + 2 * size])
            ahead_rows[e, pl.ds(first * 8, size), :] = high
            ahead_rows[e, pl.ds(L + first * 8, size), :] = low

    owner = lax.axis_index("energy")
    chosen = [jnp.int32(-1) for _ in range(slots.shape[0])]
    count = jnp.int32(0)
    for index in range(owners.shape[1]):
        hit = owners[0, index] == owner
        for c in range(len(chosen)):
            chosen[c] = jnp.where(hit & (count == c), index, chosen[c])
        count = count + hit.astype(jnp.int32)
    for c in range(len(chosen)):
        slots[c] = jnp.full(slots.shape[1:], chosen[c], jnp.int32)

    sides = []
    lowers, inverses_of = [], []
    unit = (lane_index % 8 == sub_index).astype(f32)
    inside = [spread_lane(state[0], half + n) for n in range(8)]
    for block in range(L // 8):
        column = half + block * 8
        factors = [
            [spread_lane(state[t], column + n) for n in range(8)] for t in range(block + 1, len(state))
        ]
        beside = list(factors[0]) if block < 7 else [jnp.zeros_like(unit)] * 8
        following = [spread_lane(state[block + 1], column + 8 + n) for n in range(8)] if block < 7 else []
        within = lane_index % L // 8 == block
        before = lane_index % L < block * 8
        rows = jnp.where(within, unit, state[block])
        lowers.append(jnp.where(before | within, rows, 0.0))
        if block == L // 8 - 1:
            sides = apply_left()
        for n in range(0, 8, 2):
            first, cross, second = (
                spread_row(inside[n], n), spread_row(inside[n], n + 1), spread_row(inside[n + 1], n + 1)
            )
            inverse = 1.0 / (first * second - cross * cross)
            first, cross, second = first * inverse, cross * inverse, second * inverse

            def solve(x, y):
                return second * x - cross * y, first * y - cross * x

            for m in range(n + 2, 8):
                x, y = solve(spread_row(inside[m], n), spread_row(inside[m], n + 1))
                left = inside[m] - (inside[n] * x + inside[n + 1] * y)
                inside[m] = jnp.where(sub_index == n, x, jnp.where(sub_index == n + 1, y, left))
                beside[m] = beside[m] - (beside[n] * x + beside[n + 1] * y)
            upper, lower = solve(beside[n], beside[n + 1])
            for m in range(len(following)):
                following[m] = following[m] - (
                    upper * spread_row(beside[n], m) + lower * spread_row(beside[n + 1], m)
                )
            x, y = solve(spread_row(rows, n), spread_row(rows, n + 1))
            left = rows - (inside[n] * x + inside[n + 1] * y)
            rows = jnp.where(sub_index == n, x, jnp.where(sub_index == n + 1, y, left))
        inside = following
        inverses_of.append(jnp.where(before | within, rows, 0.0))
        if block >= 1 and (block - 1) % 2 == 0:
            apply_right(block - 1, 2)
        solved = [spread_row(rows, n) for n in range(8)]
        for t in range(block + 1, len(state)):
            kept = jnp.where(within, 0.0, state[t])
            for n in range(8):
                kept = kept - factors[t - block - 1][n] * solved[n]
            state[t] = kept

    for first in ():
        apply_right(first, 2)
    for e in range(local):
        high, low = split(sides[e])
        left = jnp.concatenate([high, jnp.where(lanes < L, low, none)], 0)
        full = dot_nn(left, ahead_rows[e])
        sigma = (full[:height] + full[height:]) * (1.0 / L)
        rows = [sigma[n * 8 : n * 8 + 8].astype(bf16) for n in range(3)]
        for peer in range(out.shape[0]):
            out[peer, e] = rows[0 if peer == 0 else 1 + peer % 4 // 2]

def place_kernel(incoming, slots, out):
    groups, local, rows, columns = incoming.shape
    zeros = jnp.zeros((rows, columns), out.dtype)
    sources = [incoming[n // local, n % local].astype(f32) for n in range(groups * local)]
    for c in range(out.shape[1]):
        index = jnp.concatenate([slots[c]] * (columns // BS), 1)
        total = jnp.zeros((rows, columns), f32)
        for n, source in enumerate(sources):
            total = jnp.where(index == n, source, total)
        out[0, c, 0] = total.astype(out.dtype)
        out[0, c, 1] = zeros


def body(energies, onsite, blocks, pattern, probes, ranks, owner_map):
    local = energies.shape[0]
    groups = lax.axis_size("energy")
    rows = NC // lax.axis_size("contour")
    row_blocks = blocks.shape[0]
    vmem = pl.BlockSpec(memory_space=pltpu.VMEM)
    anywhere = pl.BlockSpec(memory_space=pl.ANY)
    arrays = (
        energies, ranks, onsite.reshape(row_blocks, BS), pattern.T, owner_map.T, probes, blocks
    )
    sigma, slots = pl.pallas_call(
        sigma_kernel,
        out_shape=(
            pltpu.VMEM((groups, local, rows, NC), bf16),
            pltpu.VMEM((local + 1, rows, BS), jnp.int32),
        ),
        in_specs=[anywhere] * len(arrays),
        out_specs=(vmem, vmem),
        scratch_shapes=[
            pltpu.SMEM(energies.shape, f32),
            pltpu.SMEM(ranks.shape, jnp.int32),
            pltpu.VMEM((row_blocks, BS), f32),
            pltpu.SMEM((KB, row_blocks), jnp.int32),
            pltpu.SMEM((1, owner_map.shape[0]), jnp.int32),
            pltpu.VMEM(probes.shape, bf16),
            pltpu.VMEM((NEAR, BS, KB * BS), bf16),
            pltpu.VMEM((NEAR, local * BS, 2 * KB * BS), bf16),
            pltpu.VMEM((NEAR, (1 + local) * L, 2 * KB * BS), bf16),
            pltpu.VMEM((4 * local * L, NC), bf16),
            pltpu.VMEM((2 * local * L, NC), bf16),
            pltpu.VMEM((NEAR * BS, BS), bf16),
            pltpu.VMEM((NEAR, BS, KB * BS), bf16),
            pltpu.VMEM((NEAR, 4 * BS, KB * BS), f32),
            pltpu.VMEM((2 * L, 2 * BS), bf16),
            pltpu.VMEM((local, 2 * L, NC), bf16),
            pltpu.SemaphoreType.DMA((6 + NEAR,)),
        ],
        compiler_params=pltpu.CompilerParams(vmem_limit_bytes=32 * 2**20),
        name="sigma",
    )(*(pltpu.with_memory_space_constraint(array, pltpu.HBM) for array in arrays))
    exchange = exchange_groups(groups, lax.axis_size("contour"))
    incoming = lax.all_to_all(sigma, ("energy", "contour"), 0, 0, axis_index_groups=exchange)
    return pl.pallas_call(
        place_kernel,
        out_shape=jax.ShapeDtypeStruct((1, local + 1, 2, rows, NC), bf16),
        in_specs=[vmem, vmem],
        out_specs=vmem,
        name="place",
    )(
        pltpu.with_memory_space_constraint(incoming, pltpu.VMEM),
        pltpu.with_memory_space_constraint(slots, pltpu.VMEM),
    )


def solution(mesh):
    placed = (P("energy"), P(), P(), P(), P(), P("energy"), P())
    return jax.shard_map(
        body,
        mesh=mesh,
        in_specs=placed,
        out_specs=P("energy", None, None, "contour", None),
        check_vma=False,
    )
```

```python
import jax
import jax.numpy as jnp
from jax import lax
from jax.experimental import pallas as pl
from jax.experimental.pallas import tpu as pltpu
from jax.sharding import PartitionSpec as P


L = 64
NC = 512
BS = 128
KB = 3
CHAIN = (0, 4, 8)
NEAR = NC // BS
f32 = jnp.float32
bf16 = jnp.bfloat16

def follow(home, step, choose):
    out = home
    for n, at in enumerate(CHAIN):
        out = choose(home == at, CHAIN[(n + step) % len(CHAIN)], out)
    return out


def other_core(group, home):
    return group % 4 // 2 * ((home > 4))


def peer_positions(group, position, choose, groups):
    core = position % 2
    home = choose((group == 0) & (core == 0), follow(position - core, -1, choose), position - core)
    parity = (core + other_core(group, home)) % 2
    out = []
    for peer in range(groups):
        place = choose(parity == 0, follow(home, 1, choose), home) if peer == 0 else home
        out.append(place + (parity + other_core(peer, home)) % 2)
    return out


def exchange_groups(groups, positions):
    found = []
    for position in range(positions):
        at = peer_positions(0, position, lambda test, yes, no: yes if test else no, groups)
        found.append([group * positions + at[group] for group in range(groups)])
    return found


def dot_nt(left, right):
    return lax.dot_general(left, right, (((1,), (1,)), ((), ())), preferred_element_type=f32)

def dot_nn(left, right):
    return lax.dot_general(left, right, (((1,), (0,)), ((), ())), preferred_element_type=f32)

def dot_tn(left, right):
    return lax.dot_general(left, right, (((0,), (0,)), ((), ())), preferred_element_type=f32)


def split(x):
    high = x.astype(bf16)
    return high, (x - high.astype(f32)).astype(bf16)

def spread_lane(x, lanes):
    return jnp.take_along_axis(x, lanes, axis=1)


def spread_row(x, row, rows=8):
    return jnp.broadcast_to(x[row : row + 1, :], (rows, x.shape[1]))


def split_wide(x):
    high = x.astype(bf16).astype(f32)
    return high, x - high


def ladder(x, exponent):
    square = x * x
    fourth = square * square
    out = jnp.where(exponent % 2 == 1, x, 1.0)
    out = jnp.where(exponent // 2 % 2 == 1, out * square, out)
    out = jnp.where(exponent // 4 == 1, out * fourth, out)
    return out, fourth * fourth


def powers(base):
    out = [base]
    for _ in range(6):
        out.append(out[-1] * out[-1])
    return out

def sigma_kernel(
    energies_in, ranks_in, onsite_in, pattern_in, owners_in, probes, blocks, out, slots,
    energies, ranks, onsite, pattern, owners, pr, bl, mix, near_terms, big, bp,
    left_rows, right_rows, products, turned, ahead_rows, sems,
):
    local = energies.shape[0]
    small_copies = [
        pltpu.make_async_copy(source, target, sems.at[n])
        for n, (source, target) in enumerate(
            (
                (onsite_in, onsite),
                (pattern_in, pattern),
                (energies_in, energies),
                (ranks_in, ranks),
                (owners_in, owners),
            )
        )
    ]
    block_copies = [
        pltpu.make_async_copy(
            blocks.at[pl.ds(0, NEAR), k], bl.at[:, :, pl.ds(k * BS, BS)], sems.at[6 + k]
        )
        for k in range(KB)
    ]
    probe_copy = pltpu.make_async_copy(probes, pr, sems.at[5])
    for copy in small_copies + block_copies + [probe_copy]:
        copy.start()
    position = lax.axis_index("contour")
    sub_index = lax.broadcasted_iota(jnp.int32, (8, BS), 0)
    lane_index = lax.broadcasted_iota(jnp.int32, (8, BS), 1)

    for copy in small_copies:
        copy.wait()
    all_weights = []
    for i in range(NEAR):
        near = spread_row(onsite[pl.ds(i, 1), :], 0, 8)
        for e in range(local):
            low_order, raised = ladder(near - energies[e], sub_index)
            high_order, _ = ladder(raised, sub_index)
            for h, table in enumerate((low_order, high_order)):
                high, low = split_wide(table)
                at = i * BS + (e * 2 + h) * 32
                left_rows[pl.ds(at, 32), :] = jnp.concatenate([high, high, low, low], 0).astype(bf16)
    def power_block(i):
        weights = []
        for k in range(KB):
            far = spread_row(onsite[pl.ds(pattern[k, i], 1), :], 0, 8)
            for e in range(local):
                low_order, raised = ladder(far - energies[e], 7 - sub_index)
                high_order, last = ladder(raised, 7 - sub_index)
                weight = 1.0 / (1.0 + last)
                weights.append(weight)
                for h, table in enumerate((low_order, high_order * weight)):
                    high, low = split_wide(table)
                    right_rows[i, pl.ds((e * 2 + h) * 32, 32), pl.ds(k * BS, BS)] = jnp.concatenate(
                        [high, low, high, low], 0
                    ).astype(bf16)
        for g in range(2 * local):
            products[i, pl.ds(g * BS, BS), :] = dot_tn(
                left_rows[pl.ds(i * BS + g * 32, 32), :], right_rows[i, pl.ds(g * 32, 32), :]
            )
        all_weights.append(weights)
    for i in range(NEAR):
        power_block(i)
    for copy in block_copies:
        copy.wait()
    def mix_block(i):
        for k in range(KB):
            for r in range(BS // 16):
                coupling = bl[i, pl.ds(r * 16, 16), pl.ds(k * BS, BS)].astype(f32)
                for e in range(local):
                    low_order = products[i, pl.ds(e * 2 * BS + r * 16, 16), pl.ds(k * BS, BS)]
                    high_order = products[i, pl.ds((e * 2 + 1) * BS + r * 16, 16), pl.ds(k * BS, BS)]
                    high, low = split(coupling * (low_order * high_order))
                    for n, part in enumerate((high, low)):
                        mix[i, pl.ds(e * BS + r * 16, 16), pl.ds((n * KB + k) * BS, BS)] = part

    def gather_terms(i):
        for k in range(KB):
            far = pr[:, pl.ds(pl.multiple_of(pattern[k, i] * BS, BS), BS)]
            for n in range(2):
                near_terms[i, pl.ds(0, L), pl.ds((n * KB + k) * BS, BS)] = far
            far = far.astype(f32).reshape(8, 8, BS)
            for e in range(local):
                scaled = far * all_weights[i][k * local + e][None]
                near_terms[i, pl.ds((1 + e) * L, L), pl.ds(k * BS, BS)] = scaled.reshape(L, BS).astype(bf16)

    def couple(i):
        return (
            dot_nt(near_terms[i, pl.ds(0, L), :], mix[i]),
            dot_nt(near_terms[i, pl.ds(L, local * L), pl.ds(0, KB * BS)], bl[i]),
        )

    def finish(i, coupled, plain):
        near = jnp.broadcast_to(onsite[pl.ds(i, 1), :], (8, BS))
        source = pr[:, pl.ds(i * BS, BS)].astype(f32).reshape(8, 8, BS)
        for e in range(local):
            mixed = coupled[:, e * BS : (e + 1) * BS].reshape(8, 8, BS)
            shift = near - energies[e]
            weight = 1.0 / (1.0 + powers(shift)[6])
            first = weight[None] * (source - mixed)
            second = shift[None] * first + plain[e * L : (e + 1) * L].reshape(8, 8, BS)
            kept = (
                lax.broadcasted_iota(jnp.int32, (8, 8, BS), 0) * 8
                + lax.broadcasted_iota(jnp.int32, (8, 8, BS), 1)
            ) < ranks[e]
            first = jnp.where(kept, first, 0.0).reshape(L, BS)
            second = jnp.where(kept, second, 0.0).reshape(L, BS)
            for n, part in enumerate(split(first) + split(second)):
                big[pl.ds((n * local + e) * L, L), pl.ds(i * BS, BS)] = part

    probe_copy.wait()
    pending = None
    for i in range(NEAR):
        mix_block(i)
        gather_terms(i)
        done = couple(i)
        if pending is not None:
            finish(i - 1, *pending)
        pending = done
    finish(NEAR - 1, *pending)

    near_high, near_low = big[pl.ds(0, BS), :], big[pl.ds(BS, BS), :]
    wide = dot_nt(near_high, big[pl.ds(0, 2 * BS), :])
    square = (wide[:, :BS] + (wide[:, BS:] + dot_nt(near_low, near_high))) * (1.0 / NC)
    far = dot_nt(big[pl.ds(0, 2 * BS), :], big[pl.ds(2 * BS, BS), :])
    across = (far[:BS] + (far[BS:] + dot_nt(near_high, big[pl.ds(3 * BS, BS), :]))) * (1.0 / NC)
    grams = []
    for e in range(local):
        grams.append(square[e * L : (e + 1) * L])
        cross = across[e * L : (e + 1) * L]
        lanes = lax.broadcasted_iota(jnp.int32, (L, BS), 1)
        high, low = split(jnp.where(lanes // L == e, cross, 0.0))
        left = jnp.concatenate(
            [jnp.concatenate([high, high], 1), jnp.concatenate([low, jnp.zeros_like(low)], 1)], 0
        )
        applied = dot_nn(left, big[pl.ds(0, 2 * BS), :])
        high, low = split(applied[:L] + applied[L:])
        bp[pl.ds(e * L, L), :] = high
        bp[pl.ds((local + e) * L, L), :] = low
    state = []
    for t in range(L // 8):
        block = jnp.where(lane_index < L, grams[0][t * 8 : t * 8 + 8], grams[1][t * 8 : t * 8 + 8])
        state.append(jnp.where(lane_index % L == sub_index + t * 8, block + 1.0, block))
    owed = peer_positions(lax.axis_index("energy"), position, jnp.where, out.shape[0])
    owed = [owed[0], owed[1], owed[2], owed[2]]
    pick = jnp.concatenate(
        [(lane_index == sub_index + lax.rem(at, BS // 8) * 8).astype(f32) for at in owed], 0
    )
    near_block = pl.multiple_of(lax.div(position, BS // 8) * BS, BS)
    mine = dot_nt(pick.astype(bf16), big[pl.ds(2 * BS, 2 * BS), pl.ds(near_block, BS)])
    mine = mine[:, :BS] + mine[:, BS:]
    half = (lane_index // L) * L

    height = 8 * len(owed)
    lanes = lax.broadcasted_iota(jnp.int32, (height, BS), 1)
    none = jnp.zeros((height, BS), bf16)

    def apply_left():
        for n, part in enumerate(split(jnp.concatenate(lowers, 0))):
            for copy in range(2):
                turned[pl.ds(copy * L, L), pl.ds(n * BS, BS)] = part
        high, low = split(mine)
        out = []
        for e in range(local):
            own = lanes // L == e
            left = jnp.concatenate(
                [
                    jnp.concatenate([jnp.where(own, high, none)] * 2, 1),
                    jnp.concatenate([jnp.where(own, low, none), none], 1),
                ],
                0,
            )
            across = dot_nt(left, turned[...])
            out.append(across[:height] + across[height:])
        return out

    def apply_right(first, count):
        tall = jnp.concatenate(inverses_of[first : first + count], 0)
        size = count * 8
        tall_lanes = lax.broadcasted_iota(jnp.int32, tall.shape, 1)
        parts = []
        for e in range(local):
            high, low = split(jnp.where(tall_lanes // L == e, tall, 0.0))
            parts.append(jnp.concatenate([high, high], 1))
            parts.append(jnp.concatenate([low, jnp.zeros_like(low)], 1))
        full = dot_nn(jnp.concatenate(parts, 0), bp[...])
        for e in range(local):
            at = 2 * e * size
            high, low = split(full[at : at + size] + full[at + size : at + 2 * size])
            ahead_rows[e, pl.ds(first * 8, size), :] = high
            ahead_rows[e, pl.ds(L + first * 8, size), :] = low

    owner = lax.axis_index("energy")
    chosen = [jnp.int32(-1) for _ in range(slots.shape[0])]
    count = jnp.int32(0)
    for index in range(owners.shape[1]):
        hit = owners[0, index] == owner
        for c in range(len(chosen)):
            chosen[c] = jnp.where(hit & (count == c), index, chosen[c])
        count = count + hit.astype(jnp.int32)
    for c in range(len(chosen)):
        slots[c] = jnp.full(slots.shape[1:], chosen[c], jnp.int32)

    sides = []
    lowers, inverses_of = [], []
    unit = (lane_index % 8 == sub_index).astype(f32)
    inside = [spread_lane(state[0], half + n) for n in range(8)]
    for block in range(L // 8):
        column = half + block * 8
        factors = [
            [spread_lane(state[t], column + n) for n in range(8)] for t in range(block + 1, len(state))
        ]
        beside = list(factors[0]) if block < 7 else [jnp.zeros_like(unit)] * 8
        following = [spread_lane(state[block + 1], column + 8 + n) for n in range(8)] if block < 7 else []
        within = lane_index % L // 8 == block
        before = lane_index % L < block * 8
        rows = jnp.where(within, unit, state[block])
        lowers.append(jnp.where(before | within, rows, 0.0))
        if block == L // 8 - 1:
            sides = apply_left()
        for n in range(0, 8, 2):
            first, cross, second = (
                spread_row(inside[n], n), spread_row(inside[n], n + 1), spread_row(inside[n + 1], n + 1)
            )
            inverse = 1.0 / (first * second - cross * cross)
            first, cross, second = first * inverse, cross * inverse, second * inverse

            def solve(x, y):
                return second * x - cross * y, first * y - cross * x

            for m in range(n + 2, 8):
                x, y = solve(spread_row(inside[m], n), spread_row(inside[m], n + 1))
                left = inside[m] - (inside[n] * x + inside[n + 1] * y)
                inside[m] = jnp.where(sub_index == n, x, jnp.where(sub_index == n + 1, y, left))
                beside[m] = beside[m] - (beside[n] * x + beside[n + 1] * y)
            upper, lower = solve(beside[n], beside[n + 1])
            for m in range(len(following)):
                following[m] = following[m] - (
                    upper * spread_row(beside[n], m) + lower * spread_row(beside[n + 1], m)
                )
            x, y = solve(spread_row(rows, n), spread_row(rows, n + 1))
            left = rows - (inside[n] * x + inside[n + 1] * y)
            rows = jnp.where(sub_index == n, x, jnp.where(sub_index == n + 1, y, left))
        inside = following
        inverses_of.append(jnp.where(before | within, rows, 0.0))
        if block >= 1 and (block - 1) % 2 == 0:
            apply_right(block - 1, 2)
        solved = [spread_row(rows, n) for n in range(8)]
        for t in range(block + 1, len(state)):
            kept = jnp.where(within, 0.0, state[t])
            for n in range(8):
                kept = kept - factors[t - block - 1][n] * solved[n]
            state[t] = kept

    for first in ():
        apply_right(first, 2)
    for e in range(local):
        high, low = split(sides[e])
        left = jnp.concatenate([high, jnp.where(lanes < L, low, none)], 0)
        full = dot_nn(left, ahead_rows[e])
        sigma = (full[:height] + full[height:]) * (1.0 / L)
        rows = [sigma[n * 8 : n * 8 + 8].astype(bf16) for n in range(3)]
        for peer in range(out.shape[0]):
            out[peer, e] = rows[0 if peer == 0 else 1 + peer % 4 // 2]

def place_kernel(incoming, slots, out):
    groups, local, rows, columns = incoming.shape
    zeros = jnp.zeros((rows, columns), out.dtype)
    sources = [incoming[n // local, n % local].astype(f32) for n in range(groups * local)]
    for c in range(out.shape[1]):
        index = jnp.concatenate([slots[c]] * (columns // BS), 1)
        total = jnp.zeros((rows, columns), f32)
        for n, source in enumerate(sources):
            total = jnp.where(index == n, source, total)
        out[0, c, 0] = total.astype(out.dtype)
        out[0, c, 1] = zeros


def body(energies, onsite, blocks, pattern, probes, ranks, owner_map):
    local = energies.shape[0]
    groups = lax.axis_size("energy")
    rows = NC // lax.axis_size("contour")
    row_blocks = blocks.shape[0]
    vmem = pl.BlockSpec(memory_space=pltpu.VMEM)
    anywhere = pl.BlockSpec(memory_space=pl.ANY)
    arrays = (
        energies, ranks, onsite.reshape(row_blocks, BS), pattern.T, owner_map.T, probes, blocks
    )
    sigma, slots = pl.pallas_call(
        sigma_kernel,
        out_shape=(
            pltpu.VMEM((groups, local, rows, NC), bf16),
            pltpu.VMEM((local + 1, rows, BS), jnp.int32),
        ),
        in_specs=[anywhere] * len(arrays),
        out_specs=(vmem, vmem),
        scratch_shapes=[
            pltpu.SMEM(energies.shape, f32),
            pltpu.SMEM(ranks.shape, jnp.int32),
            pltpu.VMEM((row_blocks, BS), f32),
            pltpu.SMEM((KB, row_blocks), jnp.int32),
            pltpu.SMEM((1, owner_map.shape[0]), jnp.int32),
            pltpu.VMEM(probes.shape, bf16),
            pltpu.VMEM((NEAR, BS, KB * BS), bf16),
            pltpu.VMEM((NEAR, local * BS, 2 * KB * BS), bf16),
            pltpu.VMEM((NEAR, (1 + local) * L, 2 * KB * BS), bf16),
            pltpu.VMEM((4 * local * L, NC), bf16),
            pltpu.VMEM((2 * local * L, NC), bf16),
            pltpu.VMEM((NEAR * BS, BS), bf16),
            pltpu.VMEM((NEAR, BS, KB * BS), bf16),
            pltpu.VMEM((NEAR, 4 * BS, KB * BS), f32),
            pltpu.VMEM((2 * L, 2 * BS), bf16),
            pltpu.VMEM((local, 2 * L, NC), bf16),
            pltpu.SemaphoreType.DMA((6 + NEAR,)),
        ],
        compiler_params=pltpu.CompilerParams(vmem_limit_bytes=32 * 2**20),
        name="sigma",
    )(*(pltpu.with_memory_space_constraint(array, pltpu.HBM) for array in arrays))
    exchange = exchange_groups(groups, lax.axis_size("contour"))
    incoming = lax.all_to_all(sigma, ("energy", "contour"), 0, 0, axis_index_groups=exchange)
    return pl.pallas_call(
        place_kernel,
        out_shape=jax.ShapeDtypeStruct((1, local + 1, 2, rows, NC), bf16),
        in_specs=[vmem, vmem],
        out_specs=vmem,
        name="place",
    )(
        pltpu.with_memory_space_constraint(incoming, pltpu.VMEM),
        pltpu.with_memory_space_constraint(slots, pltpu.VMEM),
    )


def solution(mesh):
    placed = (P("energy"), P(), P(), P(), P(), P("energy"), P())
    return jax.shard_map(
        body,
        mesh=mesh,
        in_specs=placed,
        out_specs=P("energy", None, None, "contour", None),
        check_vma=False,
    )
```
